32 devices in a mesh: grp: 4 (over y, x), tile: 8 (over z, core).
Axes of the slice: x: 2, y: 2, z: 4, core: 2. Of those that a mesh axis runs over, the one named last changes fastest.
Arguments:
- ocean: float32 [4, 32, 16, 1024], P(None, None, 'grp', 'tile'), may hold values from -3 to 3
- tracers: bfloat16 [10, 32, 16, 1024], P(None, None, 'grp', 'tile'), may hold values from -6 to 6
- wet_blocks: int32 [4, 64], P('grp', 'tile'), may hold values 0 or 1
- surface_light: float32 [16, 1024], P('grp', 'tile'), may hold values from 0.5 to 1.5
- rates: float32 [10, 10], replicated, may hold values from -2 to 2
Outputs:
- ocean_out: float32 [4, 32, 16, 1024], P(None, None, 'grp', 'tile')
- tracer_out: bfloat16 [10, 32, 16, 1024], P(None, None, 'grp', 'tile')
- heating: float32 [32, 16, 1024], P(None, 'grp', 'tile')
The draws below stay inside these ranges and needn't reach their ends.
All inputs are finite; a program needn't handle non-finite values. No bound on the sum of `wet_blocks` on one device may be relied on, other than what follows from the above.
Results may differ from the reference program's by a relative error of at most 0.0031.
Values may be sent and summed in bfloat16 or wider, within the bound.
A program may use at most 64 MiB of HBM per device.

```python
import jax
import jax.numpy as jnp
from jax import lax

NZ = 32
NTR = 10
WBY = 4
WBX = 16
NX = 1024
NY = 16


def draw_ocean(key, part):
    vel_key = jax.random.fold_in(key, 7001)
    state_key = jax.random.fold_in(key, 7002)
    shape_half = (2, NZ, NY, NX)
    velocity = jax.random.uniform(vel_key, shape_half, jnp.float32, -3.0, 3.0)
    scalars = jnp.clip(jax.random.normal(state_key, shape_half, jnp.float32), -3.0, 3.0)
    return jnp.concatenate([velocity, scalars], 0).astype(jnp.float32)


def plant(array, own_key, low, top_value):
    longest = array.shape.index(max(array.shape))
    spots = []
    for shift in (0, 1):
        where = [jax.random.randint(jax.random.fold_in(own_key, axis), (), 0, length) for axis, length in enumerate(array.shape)]
        where[longest] = (where[longest] + shift) % array.shape[longest]
        spots.append(tuple(where))
    return array.at[spots[0]].set(low).at[spots[1]].set(top_value)


def shard_levels(stream_key, extent, cuts, low, high):
    loudness, own = 1.0, jax.random.fold_in(stream_key, 6)
    for position, shards_of in cuts:
        heights = jnp.exp(jax.random.uniform(jax.random.fold_in(own, position), (shards_of,), jnp.float32, low / len(cuts), high / len(cuts)))
        loudness = loudness * jnp.repeat(heights, extent[position] // shards_of).reshape([-1 if axis == position else 1 for axis in range(len(extent))])
    return loudness


def scatter_about(key, dims, scale, most, pieces=(), held_as=jnp.bfloat16):
    array = scale * jax.random.normal(key, dims, jnp.float32)
    if pieces:
        array = array * shard_levels(key, dims, pieces, -0.22, 0.18)
    return jnp.clip(array, -most, most).astype(held_as)


def setup_inputs(seed: int = 0) -> dict:
    key_of = jax.random.split(jax.random.key(seed), 6)
    return {
        "ocean": draw_ocean(jax.random.fold_in(key_of[5], 71), 0),
        "tracers": scatter_about(key_of[1], (NTR, NZ, NY, NX), 1.0, 6.0, ((2, 4), (3, 8))),
        "wet_blocks": plant((jax.random.randint(key_of[2], (NY // WBY, NX // WBX), 0, 3) < 2).astype(jnp.int32), jax.random.fold_in(key_of[2], 1), 0, 1),
        "surface_light": jnp.clip(0.5 + 1.0 * jax.random.uniform(key_of[3], (NY, NX), jnp.float32) ** shard_levels(key_of[3], (NY, NX), ((0, 4), (1, 8)), -0.2, 0.2), 0.5, 1.5),
        "rates": scatter_about(key_of[4], (NTR, NTR), NTR ** -0.5, 2.0, (), jnp.float32),
    }


time_step = 0.3
coriolis = 0.2
viscosity = 0.1
diffusion = 0.05
thermal = 0.2
haline = 0.15
gravity_red = 0.05
react_step = 0.5
water_atten = 0.3
chloro_atten = 0.2


def minmod(first, second):
    return 0.5 * (jnp.sign(first) + jnp.sign(second)) * jnp.minimum(jnp.abs(first), jnp.abs(second))


def ocean_tendency(padded):
    center = padded[:, :, 2:-2, 2:-2]
    east_side = padded[:, :, 2:-2, 3:-1]
    west_side = padded[:, :, 2:-2, 1:-3]
    north_side = padded[:, :, 3:-1, 2:-2]
    south_side = padded[:, :, 1:-3, 2:-2]
    grad_x = 0.5 * (east_side - west_side)
    grad_y = 0.5 * (north_side - south_side)
    laplace = east_side + west_side + north_side + south_side - 4.0 * center
    zonal_vel = center[0]
    merid_vel = center[1]
    advect = -(zonal_vel[None] * grad_x + merid_vel[None] * grad_y)
    press_x = gravity_red * jnp.cumsum(thermal * grad_x[2] - haline * grad_x[3], axis=0)
    press_y = gravity_red * jnp.cumsum(thermal * grad_y[2] - haline * grad_y[3], axis=0)
    zonal_rate = advect[0] + coriolis * merid_vel - press_x + viscosity * laplace[0]
    merid_rate = advect[1] - coriolis * zonal_vel - press_y + viscosity * laplace[1]
    heat_rate = advect[2] + diffusion * laplace[2]
    salt_rate = advect[3] + diffusion * laplace[3]
    return jnp.stack([zonal_rate, merid_rate, heat_rate, salt_rate], 0)


def limited_divergence(cells, speeds, axis):
    count = cells.shape[axis] - 4

    def part(source, start, length):
        return lax.slice_in_dim(source, start, start + length, axis=axis)

    face_speed = 0.5 * (part(speeds, 1, count + 1) + part(speeds, 2, count + 1))
    behind = part(cells, 0, count + 1)
    inside = part(cells, 1, count + 1)
    ahead = part(cells, 2, count + 1)
    beyond = part(cells, 3, count + 1)
    left_value = inside + 0.5 * minmod(inside - behind, ahead - inside)
    right_value = ahead - 0.5 * minmod(ahead - inside, beyond - ahead)
    flux = jnp.maximum(face_speed, 0.0) * left_value + jnp.minimum(face_speed, 0.0) * right_value
    return part(flux, 1, count) - part(flux, 0, count)


def tracer_tendency(cells, padded_ocean):
    zonal_row = padded_ocean[0:1, :, 2:-2, :]
    merid_col = padded_ocean[1:2, :, :, 2:-2]
    along_x = limited_divergence(cells[:, :, 2:-2, :], zonal_row, 3)
    along_y = limited_divergence(cells[:, :, :, 2:-2], merid_col, 2)
    return -(along_x + along_y)


def expand_mask(wet_blocks):
    blocks = wet_blocks.astype(jnp.float32)
    rows, cols = blocks.shape
    wide = jnp.broadcast_to(blocks[:, None, :, None], (rows, WBY, cols, WBX))
    return wide.reshape(rows * WBY, cols * WBX)


def finish(ocean_two, tracer_two, wet_blocks, surface_light, rates):
    wet_cells = expand_mask(wet_blocks)
    reaction = jnp.einsum("ab,bzyx->azyx", rates, tracer_two, precision=lax.Precision.HIGHEST)
    reacted = tracer_two + react_step * wet_cells * reaction
    attenuation = water_atten + chloro_atten * reacted[0] * reacted[0]
    depth_sum = jnp.cumsum(attenuation, axis=0)
    heating = wet_cells * surface_light * (jnp.exp(attenuation - depth_sum) - jnp.exp(-depth_sum))
    ocean_out = jnp.concatenate([ocean_two[:2], ocean_two[2:3] + time_step * heating[None], ocean_two[3:]], 0)
    return ocean_out, reacted.astype(jnp.bfloat16), heating


def pad_rim(field):
    return jnp.pad(field, ((0, 0), (0, 0), (2, 2), (2, 2)))


def section_rates(ocean_state, tracer_state):
    padded_ocean = pad_rim(ocean_state)
    ocean_rate = ocean_tendency(padded_ocean)
    tracer_rate = lax.map(lambda single: tracer_tendency(pad_rim(single[None]), padded_ocean)[0], tracer_state)
    return ocean_rate, tracer_rate


def reference(ocean, tracers, wet_blocks, surface_light, rates):
    start = tracers.astype(jnp.float32)
    ocean_rate, tracer_rate = section_rates(ocean, start)
    ocean_one = ocean + time_step * ocean_rate
    tracer_one = lax.optimization_barrier((start + time_step * tracer_rate).astype(jnp.bfloat16))
    tracer_mid = tracer_one.astype(jnp.float32)
    ocean_rate, tracer_rate = section_rates(ocean_one, tracer_mid)
    ocean_two = 0.5 * (ocean + ocean_one + time_step * ocean_rate)
    tracer_two = 0.5 * (start + tracer_mid + time_step * tracer_rate)
    return finish(ocean_two, tracer_two, wet_blocks, surface_light, rates)
```

```python
import functools

import jax
import jax.numpy as jnp
from jax import lax
from jax.experimental import pallas as pl
from jax.experimental.pallas import tpu as pltpu
from jax.sharding import PartitionSpec as P

WBY = 4
WBX = 16

time_step = 0.3
coriolis = 0.2
viscosity = 0.1
diffusion = 0.05
thermal = 0.2
haline = 0.15
gravity_red = 0.05
react_step = 0.5
water_atten = 0.3
chloro_atten = 0.2

MESH = pl.DeviceIdType.MESH
F32 = jnp.float32
BF16 = jnp.bfloat16
GROUP = 8
HALO = 4
RIM = [(0, 1), (0, 2), (1, 1), (1, 2), (1, 3), (2, 1), (2, 2), (3, 1), (3, 2)]
DIRS = [(dy, dx) for dy in (-1, 0, 1) for dx in (-1, 0, 1) if (dy, dx) != (0, 0)]


def minmod(a, b):
    return jnp.maximum(jnp.minimum(a, b), 0.0) + jnp.minimum(jnp.maximum(a, b), 0.0)


def lanes(x, shift):
    return pltpu.roll(x, shift % x.shape[1], 1)


def lane_of(shape):
    return lax.broadcasted_iota(jnp.int32, shape, 1)


def depth_sum(x):
    level = lax.broadcasted_iota(jnp.int32, x.shape, 0)
    step = 1
    while step < x.shape[0]:
        x = x + jnp.where(level >= step, pltpu.roll(x, step, 0), 0.0)
        step *= 2
    return x


def over_groups(x):
    step = GROUP
    while step < x.shape[1]:
        x = x + lanes(x, step)
        step *= 2
    return x


def split_speed(speed):
    return jnp.maximum(speed, 0.0), jnp.minimum(speed, 0.0)


def kernel(ngrp, ntile, tr, oc, wet, light, rates, oc_out, tr_out, heat_out,
           halo_tr, halo_oc, send_oc, px, st, oe, o1, m1, z1, m2, z2, ua, va, ub, vb, tt,
           p_send, p_recv, o_send, o_recv, t_send, t_recv):
    ntr, ny, nz, nx = tr.shape
    gy, gx = lax.axis_index("grp"), lax.axis_index("tile")
    there = {-1: gy > 0, 0: True, 1: gy < ngrp - 1}
    over = {-1: gx > 0, 0: True, 1: gx < ntile - 1}

    def has(dy, dx):
        return jnp.logical_and(there[dy], over[dx])

    def peer(dy, dx):
        return (gy + dy, gx + dx)

    barrier = pltpu.get_barrier_semaphore()
    for dy, dx in DIRS:
        @pl.when(has(dy, dx))
        def _(dy=dy, dx=dx):
            pl.semaphore_signal(barrier, inc=1, device_id=peer(dy, dx), device_id_type=MESH)

    num_y = 1 + there[-1].astype(jnp.int32) + there[1].astype(jnp.int32)
    num_x = 1 + over[-1].astype(jnp.int32) + over[1].astype(jnp.int32)

    for slot, (field, depth) in enumerate(RIM):
        send_oc[1, slot] = oc[field, ny - depth].astype(BF16)
        send_oc[0, slot] = oc[field, depth - 1].astype(BF16)

    lane = lane_of((nz, nx))

    def pack(row, carry):
        total = jnp.zeros((nz, nx), F32)
        for field in range(ntr + 4):
            x = tr[field, row].astype(F32) if field < ntr else oc[field - ntr, row]
            total = jnp.where(lane // GROUP == field, lanes(x, GROUP * field + GROUP // 2), total)
        px[1, row + 2] = total.astype(BF16)
        return carry

    lax.fori_loop(0, ny, pack, 0)

    def edge_copy(dy, dx, index):
        rows = {-1: (2, ny + 2, 2), 0: (2, 2, ny), 1: (ny, 0, 2)}[dy]
        return pltpu.make_async_remote_copy(
            src_ref=px.at[1, pl.ds(rows[0], rows[2])], dst_ref=px.at[1 - dx, pl.ds(rows[1], rows[2])],
            send_sem=p_send.at[index], recv_sem=p_recv.at[index], device_id=peer(dy, dx), device_id_type=MESH)

    def ocean_copy(side):
        return pltpu.make_async_remote_copy(
            src_ref=send_oc.at[side], dst_ref=halo_oc.at[side],
            send_sem=o_send.at[side], recv_sem=o_recv.at[side],
            device_id=peer(2 * side - 1, 0), device_id_type=MESH)

    def tracer_copy(side, t):
        return pltpu.make_async_remote_copy(
            src_ref=tr.at[t, pl.ds(side * (ny - HALO), HALO)], dst_ref=halo_tr.at[side, t],
            send_sem=t_send.at[side, t], recv_sem=t_recv.at[side, t],
            device_id=peer(2 * side - 1, 0), device_id_type=MESH)

    pl.semaphore_wait(barrier, num_y * num_x - 1)
    for index, (dy, dx) in enumerate(DIRS):
        @pl.when(has(dy, dx))
        def _(dy=dy, dx=dx, index=index):
            edge_copy(dy, dx, index).start()
    for side in (0, 1):
        @pl.when(there[2 * side - 1])
        def _(side=side):
            ocean_copy(side).start()
    for t in range(ntr):
        for side in (0, 1):
            @pl.when(there[2 * side - 1])
            def _(side=side, t=t):
                tracer_copy(side, t).start()

    for index, (dy, dx) in enumerate(DIRS):
        @pl.when(jnp.logical_not(has(-dy, -dx)))
        def _(dy=dy, dx=dx):
            start, size = {-1: (ny + 2, 2), 0: (2, ny), 1: (0, 2)}[dy]
            px[1 - dx, pl.ds(start, size)] = jnp.zeros((size, nz, nx), BF16)
    for side in (0, 1):
        @pl.when(jnp.logical_not(there[1 - 2 * side]))
        def _(side=side):
            halo_oc[side] = jnp.zeros(halo_oc.shape[1:], BF16)
            halo_tr[side] = jnp.zeros(halo_tr.shape[1:], BF16)

    for field in range(4):
        for row in range(ny):
            oe[field, row + 3] = oc[field, row]

    for index, (dy, dx) in enumerate(DIRS):
        @pl.when(has(-dy, -dx))
        def _(dy=dy, dx=dx, index=index):
            edge_copy(dy, dx, index).wait_recv()

    part = lane % GROUP
    near_west = part == GROUP // 2

    def strips(slot, carry):
        west, own, east = (px[k, slot].astype(F32) for k in range(3))
        low = part < GROUP // 2
        left = jnp.where(low, west, own)
        right = jnp.where(low, own, east)
        st[0, slot], st[1, slot] = left, right
        mid = jnp.where(near_west, lanes(left, 1), lanes(right, -1))
        far = jnp.where(near_west, lanes(left, 2), lanes(right, -2))
        close = jnp.where(near_west, left, right)
        m1[slot] = mid
        z1[slot] = mid + 0.5 * minmod(mid - far, close - mid)
        return carry

    lax.fori_loop(0, ny + 4, strips, 0)

    group = lane // GROUP
    buoyancy = jnp.where(group == ntr + 2, thermal, 0.0) - jnp.where(group == ntr + 3, haline, 0.0)
    blend = jnp.where(group < ntr + 2, viscosity, diffusion)

    def strip_step(side, slot):
        c = [st[side, slot + k] for k in (-2, -1, 0, 1, 2)]
        mid = c[2]
        zonal = over_groups(jnp.where(group == ntr, mid, 0.0))
        merid = [over_groups(jnp.where(group == ntr + 1, x, 0.0)) for x in c[1:4]]
        east, west, north, south = lanes(mid, -1), lanes(mid, 1), c[3], c[1]
        gx_, gy_ = 0.5 * (east - west), 0.5 * (north - south)
        lap = east + west + north + south - 4.0 * mid
        px_ = gravity_red * depth_sum(over_groups(buoyancy * gx_))
        py_ = gravity_red * depth_sum(over_groups(buoyancy * gy_))
        rate = blend * lap - (zonal * gx_ + merid[1] * gy_)
        rate = rate + jnp.where(group == ntr, coriolis * merid[1] - px_, 0.0)
        rate = rate - jnp.where(group == ntr + 1, coriolis * zonal + py_, 0.0)
        ocean_one = mid + time_step * rate
        diff = mid - west
        half = 0.5 * minmod(diff, lanes(diff, -1))
        plus, minus = split_speed(0.5 * (zonal + lanes(zonal, 1)))
        flux = plus * lanes(mid + half, 1) + minus * (mid - half)
        div = lanes(flux, -1) - flux
        d = [c[k + 1] - c[k] for k in range(4)]
        h = [0.5 * minmod(d[k], d[k + 1]) for k in range(3)]
        fluxes = []
        for k in (0, 1):
            plus, minus = split_speed(0.5 * (merid[k] + merid[k + 1]))
            fluxes.append(plus * (c[k + 1] + h[k]) + minus * (c[k + 2] - h[k + 1]))
        div = div + (fluxes[1] - fluxes[0])
        tracer_one = (mid - time_step * div).astype(BF16).astype(F32)
        return jnp.where(group < ntr, tracer_one, ocean_one)

    in_west = jnp.where(over[-1], 1.0, 0.0)
    in_east = jnp.where(over[1], 1.0, 0.0)

    def strip_row(row, carry):
        left = strip_step(0, row + 2)
        right = strip_step(1, row + 2)
        mid = jnp.where(near_west, in_west * lanes(left, 1), in_east * lanes(right, -1))
        far = jnp.where(near_west, in_west * lanes(left, 2), in_east * lanes(right, -2))
        close = jnp.where(near_west, left, right)
        m2[row] = mid
        z2[row] = mid + 0.5 * minmod(mid - far, close - mid)
        return carry

    lax.fori_loop(0, ny, strip_row, 0)

    for side in (0, 1):
        @pl.when(there[1 - 2 * side])
        def _(side=side):
            ocean_copy(side).wait_recv()
    for slot, (field, depth) in enumerate(RIM):
        oe[field, 3 - depth] = halo_oc[1, slot].astype(F32)
        oe[field, ny + 2 + depth] = halo_oc[0, slot].astype(F32)

    first, last = lane == 0, lane == nx - 1

    def shift_back(field):
        return -(GROUP * field + GROUP // 2)

    def ocean_rates(get, edge):
        center = [get(f, 0) for f in range(4)]
        zonal, merid = center[0], center[1]
        rates_, grads = [], []
        for f in range(4):
            mid = center[f]
            rim = lanes(edge, shift_back(ntr + f))
            east = jnp.where(last, rim, lanes(mid, -1))
            west = jnp.where(first, rim, lanes(mid, 1))
            north, south = get(f, 1), get(f, -1)
            gx_, gy_ = 0.5 * (east - west), 0.5 * (north - south)
            lap = east + west + north + south - 4.0 * mid
            rates_.append((viscosity if f < 2 else diffusion) * lap - (zonal * gx_ + merid * gy_))
            grads.append((gx_, gy_))
        px_, py_ = (gravity_red * depth_sum(thermal * grads[2][k] - haline * grads[3][k]) for k in (0, 1))
        rates_[0] = rates_[0] + coriolis * merid - px_
        rates_[1] = rates_[1] - coriolis * zonal - py_
        return rates_

    in_south = jnp.where(there[-1], 1.0, 0.0)
    in_north = jnp.where(there[1], 1.0, 0.0)

    def ocean_first(k, carry):
        keep = jnp.where(k == 0, in_south, jnp.where(k == ny + 1, in_north, 1.0))
        rate = ocean_rates(lambda f, dy: oe[f, k + 2 + dy], m1[k + 1])
        for f in range(4):
            o1[f, k] = keep * (oe[f, k + 2] + time_step * rate[f])
        return carry

    lax.fori_loop(0, ny + 2, ocean_first, 0)

    def ocean_second(row, carry):
        rate = ocean_rates(lambda f, dy: o1[f, row + 1 + dy], m2[row])
        for f in range(4):
            oc_out[f, row] = 0.5 * (oe[f, row + 3] + o1[f, row + 1] + time_step * rate[f])
        return carry

    lax.fori_loop(0, ny, ocean_second, 0)

    def zonal_faces(scale, mid, edge):
        rim = lanes(edge, shift_back(ntr))
        east = jnp.where(last, rim, lanes(mid, -1))
        west = jnp.where(first, rim, lanes(mid, 1))
        return split_speed(scale * (west + mid)) + split_speed(scale * (mid + east))

    def faces_first(j, carry):
        for k, x in enumerate(zonal_faces(0.5 * time_step, oe[0, j + 1], m1[j])):
            ua[k, j] = x
        return carry

    lax.fori_loop(0, ny + 4, faces_first, 0)

    def faces_second(j, carry):
        for k, x in enumerate(zonal_faces(0.25 * time_step, o1[0, j + 1], m2[j])):
            ub[k, j] = x
        return carry

    lax.fori_loop(0, ny, faces_second, 0)

    def merid_first(j, carry):
        va[0, j], va[1, j] = split_speed((0.5 * time_step) * (oe[1, j] + oe[1, j + 1]))
        return carry

    lax.fori_loop(0, ny + 5, merid_first, 0)

    def merid_second(j, carry):
        vb[0, j], vb[1, j] = split_speed((0.25 * time_step) * (o1[1, j] + o1[1, j + 1]))
        return carry

    lax.fori_loop(0, ny + 1, merid_second, 0)

    chunk = 16
    clane = lane_of((chunk, nx))
    cfirst, clast = clane == 0, clane == nx - 1

    def zonal_part(c, rim, rim_value, speeds):
        diff = c - jnp.where(cfirst, rim, lanes(c, 1))
        ahead = jnp.where(clast, rim - c, lanes(diff, -1))
        half = 0.5 * minmod(diff, ahead)
        left, right = c + half, c - half
        before = jnp.where(cfirst, rim_value, lanes(left, 1))
        after = jnp.where(clast, rim_value, lanes(right, -1))
        return (speeds[2] * left + speeds[3] * after) - (speeds[0] * before + speeds[1] * right)

    def merid_part(c, speeds):
        d = [b - a for a, b in zip(c[:-1], c[1:])]
        h = [0.5 * minmod(a, b) for a, b in zip(d[:-1], d[1:])]
        flux = []
        for k in range(len(h) - 1):
            plus, minus = speeds(k)
            flux.append(plus * (c[k + 1] + h[k]) + minus * (c[k + 2] - h[k + 1]))
        return [b - a for a, b in zip(flux[:-1], flux[1:])]

    def tracer(t, carry):
        for side in (0, 1):
            @pl.when(there[1 - 2 * side])
            def _(side=side):
                tracer_copy(side, t).wait_recv()
        back = nx - (GROUP * t + GROUP // 2)

        def levels(zc, inner):
            zs = pl.ds(pl.multiple_of(zc * chunk, chunk), chunk)
            c = [halo_tr[1, t, k, zs].astype(F32) for k in range(HALO)]
            c += [tr[t, k, zs].astype(F32) for k in range(ny)]
            c += [halo_tr[0, t, k, zs].astype(F32) for k in range(HALO)]
            along_y = merid_part(c, lambda k: (va[0, k, zs], va[1, k, zs]))
            one = []
            for j in range(ny + 4):
                rim = pltpu.roll(m1[j, zs], back, 1)
                rim_value = pltpu.roll(z1[j, zs], back, 1)
                mid = c[j + 2]
                div = zonal_part(mid, rim, rim_value, [ua[k, j, zs] for k in range(4)]) + along_y[j]
                new = (mid - div).astype(BF16).astype(F32)
                if j < 2:
                    new = in_south * new
                if j >= ny + 2:
                    new = in_north * new
                one.append(new)
            along_y = merid_part(one, lambda k: (vb[0, k, zs], vb[1, k, zs]))
            for j in range(ny):
                rim = pltpu.roll(m2[j, zs], back, 1)
                rim_value = pltpu.roll(z2[j, zs], back, 1)
                mid = one[j + 2]
                div = zonal_part(mid, rim, rim_value, [ub[k, j, zs] for k in range(4)]) + along_y[j]
                tt[t, j, zs] = 0.5 * (c[j + 4] + mid) - div
            return inner

        lax.fori_loop(0, nz // chunk, levels, 0)
        return carry

    lax.fori_loop(0, ntr, tracer, 0)

    def react(row, carry):
        mask = wet[pl.ds(row, 1), :]

        def levels(zc, inner):
            zs = pl.ds(pl.multiple_of(zc * chunk, chunk), chunk)
            x = [tt[t, row, zs] for t in range(ntr)]
            for a in range(ntr):
                total = rates[a, 0] * x[0]
                for b in range(1, ntr):
                    total = total + rates[a, b] * x[b]
                reacted = x[a] + (react_step * mask) * total
                tr_out[a, row, zs] = reacted.astype(BF16)
                if a == 0:
                    heat_out[row, zs] = water_atten + chloro_atten * reacted * reacted
            return inner

        lax.fori_loop(0, nz // chunk, levels, 0)
        att = heat_out[row]
        cum = depth_sum(att)
        heating = (mask * light[pl.ds(row, 1), :]) * (jnp.exp(att - cum) - jnp.exp(-cum))
        heat_out[row] = heating
        oc_out[2, row] = oc_out[2, row] + time_step * heating
        return carry

    lax.fori_loop(0, ny, react, 0)

    for index, (dy, dx) in enumerate(DIRS):
        @pl.when(has(dy, dx))
        def _(dy=dy, dx=dx, index=index):
            edge_copy(dy, dx, index).wait_send()
    for side in (0, 1):
        @pl.when(there[2 * side - 1])
        def _(side=side):
            ocean_copy(side).wait_send()
            for t in range(ntr):
                tracer_copy(side, t).wait_send()


def expand_mask(wet_blocks):
    blocks = wet_blocks.astype(F32)
    rows, cols = blocks.shape
    wide = jnp.broadcast_to(blocks[:, None, :, None], (rows, WBY, cols, WBX))
    return wide.reshape(rows * WBY, cols * WBX)


def shards(ngrp, ntile, ocean, tracers, wet_blocks, surface_light, rates):
    ntr, nz, ny, nx = tracers.shape
    vmem = pl.BlockSpec(memory_space=pltpu.VMEM)
    level = (nz, nx)
    outs = pl.pallas_call(
        functools.partial(kernel, ngrp, ntile),
        out_shape=(
            jax.ShapeDtypeStruct((4, ny) + level, F32),
            jax.ShapeDtypeStruct((ntr, ny) + level, BF16),
            jax.ShapeDtypeStruct((ny,) + level, F32),
        ),
        in_specs=[vmem] * 4 + [pl.BlockSpec(memory_space=pltpu.SMEM)],
        out_specs=(vmem,) * 3,
        scratch_shapes=[
            pltpu.VMEM((2, ntr, HALO) + level, BF16),
            pltpu.VMEM((2, len(RIM)) + level, BF16),
            pltpu.VMEM((2, len(RIM)) + level, BF16),
            pltpu.VMEM((3, ny + 4) + level, BF16),
            pltpu.VMEM((2, ny + 4) + level, F32),
            pltpu.VMEM((4, ny + 6) + level, F32),
            pltpu.VMEM((4, ny + 2) + level, F32),
            pltpu.VMEM((ny + 4,) + level, F32),
            pltpu.VMEM((ny + 4,) + level, F32),
            pltpu.VMEM((ny,) + level, F32),
            pltpu.VMEM((ny,) + level, F32),
            pltpu.VMEM((4, ny + 4) + level, F32),
            pltpu.VMEM((2, ny + 5) + level, F32),
            pltpu.VMEM((4, ny) + level, F32),
            pltpu.VMEM((2, ny + 1) + level, F32),
            pltpu.VMEM((ntr, ny) + level, F32),
            pltpu.SemaphoreType.DMA((len(DIRS),)),
            pltpu.SemaphoreType.DMA((len(DIRS),)),
            pltpu.SemaphoreType.DMA((2,)),
            pltpu.SemaphoreType.DMA((2,)),
            pltpu.SemaphoreType.DMA((2, ntr)),
            pltpu.SemaphoreType.DMA((2, ntr)),
        ],
        compiler_params=pltpu.CompilerParams(
            collective_id=0, has_side_effects=True, vmem_limit_bytes=24 * 1024 * 1024
        ),
    )(jnp.swapaxes(tracers, 1, 2), jnp.swapaxes(ocean, 1, 2), expand_mask(wet_blocks), surface_light, rates)
    return jnp.swapaxes(outs[0], 1, 2), jnp.swapaxes(outs[1], 1, 2), jnp.swapaxes(outs[2], 0, 1)


def solution(mesh):
    return jax.shard_map(
        functools.partial(shards, mesh.shape["grp"], mesh.shape["tile"]),
        mesh=mesh,
        in_specs=(
            P(None, None, "grp", "tile"),
            P(None, None, "grp", "tile"),
            P("grp", "tile"),
            P("grp", "tile"),
            P(),
        ),
        out_specs=(
            P(None, None, "grp", "tile"),
            P(None, None, "grp", "tile"),
            P(None, "grp", "tile"),
        ),
        check_vma=False,
    )
```

```python
import functools

import jax
import jax.numpy as jnp
from jax import lax
from jax.experimental import pallas as pl
from jax.experimental.pallas import tpu as pltpu
from jax.sharding import PartitionSpec as P

WBY = 4
WBX = 16

time_step = 0.3
coriolis = 0.2
viscosity = 0.1
diffusion = 0.05
thermal = 0.2
haline = 0.15
gravity_red = 0.05
react_step = 0.5
water_atten = 0.3
chloro_atten = 0.2

MESH = pl.DeviceIdType.MESH
F32 = jnp.float32
BF16 = jnp.bfloat16
GROUP = 8
HALO = 4
RIM = [(0, 1), (0, 2), (1, 1), (1, 2), (1, 3), (2, 1), (2, 2), (3, 1), (3, 2)]
DIRS = [(dy, dx) for dy in (-1, 0, 1) for dx in (-1, 0, 1) if (dy, dx) != (0, 0)]


def minmod(a, b):
    return jnp.maximum(jnp.minimum(a, b), 0.0) + jnp.minimum(jnp.maximum(a, b), 0.0)


def lanes(x, shift):
    return pltpu.roll(x, shift % x.shape[1], 1)


def lane_of(shape):
    return lax.broadcasted_iota(jnp.int32, shape, 1)


def depth_sum(x):
    level = lax.broadcasted_iota(jnp.int32, x.shape, 0)
    step = 1
    while step < x.shape[0]:
        x = x + jnp.where(level >= step, pltpu.roll(x, step, 0), 0.0)
        step *= 2
    return x


def loop(steps, at_once, body):
    at_once = at_once if steps % at_once == 0 else 1

    def some(i, carry):
        for k in range(at_once):
            body(at_once * i + k)
        return carry

    if steps == at_once:
        some(0, 0)
    else:
        lax.fori_loop(0, steps // at_once, some, 0)


def split_speed(speed):
    return jnp.maximum(speed, 0.0), jnp.minimum(speed, 0.0)


def kernel(ngrp, ntile, tr, oc, wet, light, rates, oc_out, tr_out, heat_out,
           halo_tr, halo_oc, send_oc, px, st, wind, oe, o1, m1, z1, m2, z2, ua, va, ub, vb, tt,
           p_send, p_recv, o_send, o_recv, t_send, t_recv, f_send):
    ntr, ny, nz, nx = tr.shape
    gy, gx = lax.axis_index("grp"), lax.axis_index("tile")
    there = {-1: gy > 0, 0: True, 1: gy < ngrp - 1}
    over = {-1: gx > 0, 0: True, 1: gx < ntile - 1}

    def has(dy, dx):
        return jnp.logical_and(there[dy], over[dx])

    def peer(dy, dx):
        return (gy + dy, gx + dx)

    barrier = pltpu.get_barrier_semaphore()
    for dy, dx in DIRS:
        @pl.when(has(dy, dx))
        def _(dy=dy, dx=dx):
            pl.semaphore_signal(barrier, inc=1, device_id=peer(dy, dx), device_id_type=MESH)

    relay = ngrp % 4 == 0 and ny == HALO
    place = gy % 4
    partner = (jnp.where(place < 2, gy + 2, gy - 2), gx)
    if relay:
        pl.semaphore_signal(barrier, inc=1, device_id=partner, device_id_type=MESH)

    num_y = 1 + there[-1].astype(jnp.int32) + there[1].astype(jnp.int32)
    num_x = 1 + over[-1].astype(jnp.int32) + over[1].astype(jnp.int32)

    for slot, (field, depth) in enumerate(RIM):
        send_oc[1, slot] = oc[field, ny - depth].astype(BF16)
        send_oc[0, slot] = oc[field, depth - 1].astype(BF16)

    lane = lane_of((nz, nx))

    def pack(row):
        total = jnp.zeros((nz, nx), F32)
        for field in range(ntr + 4):
            x = tr[field, row].astype(F32) if field < ntr else oc[field - ntr, row]
            total = jnp.where(lane // GROUP == field, lanes(x, GROUP * field + GROUP // 2), total)
        px[1, row + 2] = total.astype(BF16)

    loop(ny, 1, pack)

    def edge_copy(dy, dx, index):
        rows = {-1: (2, ny + 2, 2), 0: (2, 2, ny), 1: (ny, 0, 2)}[dy]
        return pltpu.make_async_remote_copy(
            src_ref=px.at[1, pl.ds(rows[0], rows[2])], dst_ref=px.at[1 - dx, pl.ds(rows[1], rows[2])],
            send_sem=p_send.at[index], recv_sem=p_recv.at[index], device_id=peer(dy, dx), device_id_type=MESH)

    def ocean_copy(side):
        return pltpu.make_async_remote_copy(
            src_ref=send_oc.at[side], dst_ref=halo_oc.at[side],
            send_sem=o_send.at[side], recv_sem=o_recv.at[side],
            device_id=peer(2 * side - 1, 0), device_id_type=MESH)

    def tracer_copy(side, t):
        return pltpu.make_async_remote_copy(
            src_ref=tr.at[t, pl.ds(side * (ny - HALO), HALO)], dst_ref=halo_tr.at[side, t],
            send_sem=t_send.at[side, t], recv_sem=t_recv.at[side, t],
            device_id=peer(2 * side - 1, 0), device_id_type=MESH)

    def forward_copy(side, t):
        return pltpu.make_async_remote_copy(
            src_ref=halo_tr.at[side, t], dst_ref=halo_tr.at[1 - side, t],
            send_sem=f_send.at[t], recv_sem=t_recv.at[1 - side, t], device_id=partner, device_id_type=MESH)

    def sends(side):
        direct = there[2 * side - 1]
        return jnp.logical_and(direct, place != 2 - side) if relay else direct

    def forwards(side):
        return place == 3 * side

    def forward(t):
        if relay:
            for side in (0, 1):
                @pl.when(forwards(side))
                def _(side=side):
                    tracer_copy(side, t).wait_recv()
                    forward_copy(side, t).start()

    pl.semaphore_wait(barrier, num_y * num_x - 1 + (1 if relay else 0))
    for index, (dy, dx) in enumerate(DIRS):
        @pl.when(has(dy, dx))
        def _(dy=dy, dx=dx, index=index):
            edge_copy(dy, dx, index).start()
    for side in (0, 1):
        @pl.when(there[2 * side - 1])
        def _(side=side):
            ocean_copy(side).start()
    for t in range(ntr):
        for side in (0, 1):
            @pl.when(sends(side))
            def _(side=side, t=t):
                tracer_copy(side, t).start()

    for index, (dy, dx) in enumerate(DIRS):
        @pl.when(jnp.logical_not(has(-dy, -dx)))
        def _(dy=dy, dx=dx):
            start, size = {-1: (ny + 2, 2), 0: (2, ny), 1: (0, 2)}[dy]
            px[1 - dx, pl.ds(start, size)] = jnp.zeros((size, nz, nx), BF16)
    for side in (0, 1):
        @pl.when(jnp.logical_not(there[1 - 2 * side]))
        def _(side=side):
            halo_oc[side] = jnp.zeros(halo_oc.shape[1:], BF16)
            halo_tr[side] = jnp.zeros(halo_tr.shape[1:], BF16)

    for field in range(4):
        for row in range(ny):
            oe[field, row + 3] = oc[field, row]

    for index, (dy, dx) in enumerate(DIRS):
        @pl.when(has(-dy, -dx))
        def _(dy=dy, dx=dx, index=index):
            edge_copy(dy, dx, index).wait_recv()

    part = lane % GROUP
    near_west = part == GROUP // 2

    group = lane // GROUP
    source = lax.broadcasted_iota(jnp.int32, (nx, 2 * nx), 0)
    target = lax.broadcasted_iota(jnp.int32, (nx, 2 * nx), 1)
    spread = jnp.logical_and(source // GROUP == ntr + target // nx, source % GROUP == target % GROUP)
    spread = jnp.where(spread, 1.0, 0.0).astype(BF16)

    def strips(slot):
        west, own, east = (px[k, slot].astype(F32) for k in range(3))
        low = part < GROUP // 2
        left = jnp.where(low, west, own)
        right = jnp.where(low, own, east)
        st[0, slot], st[1, slot] = left, right
        for side, x in enumerate((left, right)):
            both = jnp.dot(x.astype(BF16), spread, preferred_element_type=F32)
            wind[side, 0, slot], wind[side, 1, slot] = both[:, :nx], both[:, nx:]
        mid = jnp.where(near_west, lanes(left, 1), lanes(right, -1))
        far = jnp.where(near_west, lanes(left, 2), lanes(right, -2))
        close = jnp.where(near_west, left, right)
        m1[slot] = mid
        z1[slot] = mid + 0.5 * minmod(mid - far, close - mid)

    loop(ny + 4, 4, strips)
    forward(0)

    blend = jnp.where(group < ntr + 2, viscosity, diffusion)

    def strip_step(side, slot):
        c = [st[side, slot + k] for k in (-2, -1, 0, 1, 2)]
        mid = c[2]
        zonal = wind[side, 0, slot]
        merid = [wind[side, 1, slot + k] for k in (-1, 0, 1)]
        east, west, north, south = lanes(mid, -1), lanes(mid, 1), c[3], c[1]
        gx_, gy_ = 0.5 * (east - west), 0.5 * (north - south)
        lap = east + west + north + south - 4.0 * mid
        force = jnp.where(group == ntr, thermal * lanes(gx_, -2 * GROUP) - haline * lanes(gx_, -3 * GROUP),
                          thermal * lanes(gy_, -GROUP) - haline * lanes(gy_, -2 * GROUP))
        press = gravity_red * depth_sum(force)
        rate = blend * lap - (zonal * gx_ + merid[1] * gy_)
        rate = rate + jnp.where(group == ntr, coriolis * merid[1] - press, 0.0)
        rate = rate - jnp.where(group == ntr + 1, coriolis * zonal + press, 0.0)
        ocean_one = mid + time_step * rate
        diff = mid - west
        half = 0.5 * minmod(diff, lanes(diff, -1))
        plus, minus = split_speed(0.5 * (zonal + lanes(zonal, 1)))
        flux = plus * lanes(mid + half, 1) + minus * (mid - half)
        div = lanes(flux, -1) - flux
        d = [c[k + 1] - c[k] for k in range(4)]
        h = [0.5 * minmod(d[k], d[k + 1]) for k in range(3)]
        fluxes = []
        for k in (0, 1):
            plus, minus = split_speed(0.5 * (merid[k] + merid[k + 1]))
            fluxes.append(plus * (c[k + 1] + h[k]) + minus * (c[k + 2] - h[k + 1]))
        div = div + (fluxes[1] - fluxes[0])
        tracer_one = (mid - time_step * div).astype(BF16).astype(F32)
        return jnp.where(group < ntr, tracer_one, ocean_one)

    in_west = jnp.where(over[-1], 1.0, 0.0)
    in_east = jnp.where(over[1], 1.0, 0.0)

    def strip_row(row):
        left = strip_step(0, row + 2)
        right = strip_step(1, row + 2)
        mid = jnp.where(near_west, in_west * lanes(left, 1), in_east * lanes(right, -1))
        far = jnp.where(near_west, in_west * lanes(left, 2), in_east * lanes(right, -2))
        close = jnp.where(near_west, left, right)
        m2[row] = mid
        z2[row] = mid + 0.5 * minmod(mid - far, close - mid)

    loop(ny, 2, strip_row)
    forward(1)

    for side in (0, 1):
        @pl.when(there[1 - 2 * side])
        def _(side=side):
            ocean_copy(side).wait_recv()
    for slot, (field, depth) in enumerate(RIM):
        oe[field, 3 - depth] = halo_oc[1, slot].astype(F32)
        oe[field, ny + 2 + depth] = halo_oc[0, slot].astype(F32)

    first, last = lane == 0, lane == nx - 1

    def shift_back(field):
        return -(GROUP * field + GROUP // 2)

    def ocean_rates(get, edge):
        center = [get(f, 0) for f in range(4)]
        zonal, merid = center[0], center[1]
        rates_, grads = [], []
        for f in range(4):
            mid = center[f]
            rim = lanes(edge, shift_back(ntr + f))
            east = jnp.where(last, rim, lanes(mid, -1))
            west = jnp.where(first, rim, lanes(mid, 1))
            north, south = get(f, 1), get(f, -1)
            gx_, gy_ = 0.5 * (east - west), 0.5 * (north - south)
            lap = east + west + north + south - 4.0 * mid
            rates_.append((viscosity if f < 2 else diffusion) * lap - (zonal * gx_ + merid * gy_))
            grads.append((gx_, gy_))
        px_, py_ = (gravity_red * depth_sum(thermal * grads[2][k] - haline * grads[3][k]) for k in (0, 1))
        rates_[0] = rates_[0] + coriolis * merid - px_
        rates_[1] = rates_[1] - coriolis * zonal - py_
        return rates_

    in_south = jnp.where(there[-1], 1.0, 0.0)
    in_north = jnp.where(there[1], 1.0, 0.0)

    def ocean_first(k):
        keep = jnp.where(k == 0, in_south, jnp.where(k == ny + 1, in_north, 1.0))
        rate = ocean_rates(lambda f, dy: oe[f, k + 2 + dy], m1[k + 1])
        for f in range(4):
            o1[f, k] = keep * (oe[f, k + 2] + time_step * rate[f])

    loop(ny + 2, 2, ocean_first)
    for t in (2, 3):
        forward(t)

    def ocean_second(row):
        rate = ocean_rates(lambda f, dy: o1[f, row + 1 + dy], m2[row])
        for f in range(4):
            oc_out[f, row] = 0.5 * (oe[f, row + 3] + o1[f, row + 1] + time_step * rate[f])

    loop(ny, 2, ocean_second)
    forward(4)

    def zonal_faces(scale, mid, edge):
        rim = lanes(edge, shift_back(ntr))
        east = jnp.where(last, rim, lanes(mid, -1))
        west = jnp.where(first, rim, lanes(mid, 1))
        return split_speed(scale * (west + mid)) + split_speed(scale * (mid + east))

    def faces_first(j):
        for k, x in enumerate(zonal_faces(0.5 * time_step, oe[0, j + 1], m1[j])):
            ua[k, j] = x

    loop(ny + 4, 4, faces_first)

    def faces_second(j):
        for k, x in enumerate(zonal_faces(0.25 * time_step, o1[0, j + 1], m2[j])):
            ub[k, j] = x

    loop(ny, 4, faces_second)

    def merid_first(j):
        va[0, j], va[1, j] = split_speed((0.5 * time_step) * (oe[1, j] + oe[1, j + 1]))

    loop(ny + 5, 3, merid_first)

    def merid_second(j):
        vb[0, j], vb[1, j] = split_speed((0.25 * time_step) * (o1[1, j] + o1[1, j + 1]))

    loop(ny + 1, 5, merid_second)

    forward(5)
    ahead = 6
    chunk = 16
    clane = lane_of((chunk, nx))
    cfirst, clast = clane == 0, clane == nx - 1

    def zonal_part(c, rim, rim_value, speeds):
        diff = c - jnp.where(cfirst, rim, lanes(c, 1))
        ahead = jnp.where(clast, rim - c, lanes(diff, -1))
        half = 0.5 * minmod(diff, ahead)
        left, right = c + half, c - half
        before = jnp.where(cfirst, rim_value, lanes(left, 1))
        after = jnp.where(clast, rim_value, lanes(right, -1))
        return (speeds[2] * left + speeds[3] * after) - (speeds[0] * before + speeds[1] * right)

    def merid_part(c, speeds):
        d = [b - a for a, b in zip(c[:-1], c[1:])]
        h = [0.5 * minmod(a, b) for a, b in zip(d[:-1], d[1:])]
        flux = []
        for k in range(len(h) - 1):
            plus, minus = speeds(k)
            flux.append(plus * (c[k + 1] + h[k]) + minus * (c[k + 2] - h[k + 1]))
        return [b - a for a, b in zip(flux[:-1], flux[1:])]

    def tracer(t, carry):
        for side in (0, 1):
            arrives = there[1 - 2 * side]
            if relay:
                arrives = jnp.logical_and(arrives, jnp.logical_not(forwards(side)))

            @pl.when(arrives)
            def _(side=side):
                tracer_copy(side, t).wait_recv()
        back = nx - (GROUP * t + GROUP // 2)

        def levels(zc):
            zs = pl.ds(zc * chunk, chunk)
            c = [halo_tr[1, t, k, zs].astype(F32) for k in range(HALO)]
            c += [tr[t, k, zs].astype(F32) for k in range(ny)]
            c += [halo_tr[0, t, k, zs].astype(F32) for k in range(HALO)]
            along_y = merid_part(c, lambda k: (va[0, k, zs], va[1, k, zs]))
            one = []
            for j in range(ny + 4):
                rim = pltpu.roll(m1[j, zs], back, 1)
                rim_value = pltpu.roll(z1[j, zs], back, 1)
                mid = c[j + 2]
                div = zonal_part(mid, rim, rim_value, [ua[k, j, zs] for k in range(4)]) + along_y[j]
                new = (mid - div).astype(BF16).astype(F32)
                if j < 2:
                    new = in_south * new
                if j >= ny + 2:
                    new = in_north * new
                one.append(new)
            along_y = merid_part(one, lambda k: (vb[0, k, zs], vb[1, k, zs]))
            for j in range(ny):
                rim = pltpu.roll(m2[j, zs], back, 1)
                rim_value = pltpu.roll(z2[j, zs], back, 1)
                mid = one[j + 2]
                div = zonal_part(mid, rim, rim_value, [ub[k, j, zs] for k in range(4)]) + along_y[j]
                tt[t, j, zs] = 0.5 * (c[j + 4] + mid) - div

        for zc in range(nz // chunk):
            levels(zc)
        if relay:
            @pl.when(t + ahead < ntr)
            def _():
                forward(t + ahead)
        return carry

    lax.fori_loop(0, ntr, tracer, 0)

    def react(row, carry):
        mask = wet[pl.ds(row, 1), :]

        def levels(zc, inner):
            zs = pl.ds(pl.multiple_of(zc * chunk, chunk), chunk)
            x = [tt[t, row, zs] for t in range(ntr)]
            for a in range(ntr):
                total = rates[a, 0] * x[0]
                for b in range(1, ntr):
                    total = total + rates[a, b] * x[b]
                reacted = x[a] + (react_step * mask) * total
                tr_out[a, row, zs] = reacted.astype(BF16)
                if a == 0:
                    heat_out[row, zs] = water_atten + chloro_atten * reacted * reacted
            return inner

        lax.fori_loop(0, nz // chunk, levels, 0)
        att = heat_out[row]
        cum = depth_sum(att)
        heating = (mask * light[pl.ds(row, 1), :]) * (jnp.exp(att - cum) - jnp.exp(-cum))
        heat_out[row] = heating
        oc_out[2, row] = oc_out[2, row] + time_step * heating
        return carry

    lax.fori_loop(0, ny, react, 0)

    for index, (dy, dx) in enumerate(DIRS):
        @pl.when(has(dy, dx))
        def _(dy=dy, dx=dx, index=index):
            edge_copy(dy, dx, index).wait_send()
    for side in (0, 1):
        @pl.when(there[2 * side - 1])
        def _(side=side):
            ocean_copy(side).wait_send()

        @pl.when(sends(side))
        def _(side=side):
            for t in range(ntr):
                tracer_copy(side, t).wait_send()

        if relay:
            @pl.when(forwards(side))
            def _(side=side):
                for t in range(ntr):
                    forward_copy(side, t).wait_send()


def expand_mask(wet_blocks):
    blocks = wet_blocks.astype(F32)
    rows, cols = blocks.shape
    wide = jnp.broadcast_to(blocks[:, None, :, None], (rows, WBY, cols, WBX))
    return wide.reshape(rows * WBY, cols * WBX)


def shards(ngrp, ntile, ocean, tracers, wet_blocks, surface_light, rates):
    ntr, nz, ny, nx = tracers.shape
    vmem = pl.BlockSpec(memory_space=pltpu.VMEM)
    level = (nz, nx)
    outs = pl.pallas_call(
        functools.partial(kernel, ngrp, ntile),
        out_shape=(
            jax.ShapeDtypeStruct((4, ny) + level, F32),
            jax.ShapeDtypeStruct((ntr, ny) + level, BF16),
            jax.ShapeDtypeStruct((ny,) + level, F32),
        ),
        in_specs=[vmem] * 4 + [pl.BlockSpec(memory_space=pltpu.SMEM)],
        out_specs=(vmem,) * 3,
        scratch_shapes=[
            pltpu.VMEM((2, ntr, HALO) + level, BF16),
            pltpu.VMEM((2, len(RIM)) + level, BF16),
            pltpu.VMEM((2, len(RIM)) + level, BF16),
            pltpu.VMEM((3, ny + 4) + level, BF16),
            pltpu.VMEM((2, ny + 4) + level, F32),
            pltpu.VMEM((2, 2, ny + 4) + level, F32),
            pltpu.VMEM((4, ny + 6) + level, F32),
            pltpu.VMEM((4, ny + 2) + level, F32),
            pltpu.VMEM((ny + 4,) + level, F32),
            pltpu.VMEM((ny + 4,) + level, F32),
            pltpu.VMEM((ny,) + level, F32),
            pltpu.VMEM((ny,) + level, F32),
            pltpu.VMEM((4, ny + 4) + level, F32),
            pltpu.VMEM((2, ny + 5) + level, F32),
            pltpu.VMEM((4, ny) + level, F32),
            pltpu.VMEM((2, ny + 1) + level, F32),
            pltpu.VMEM((ntr, ny) + level, F32),
            pltpu.SemaphoreType.DMA((len(DIRS),)),
            pltpu.SemaphoreType.DMA((len(DIRS),)),
            pltpu.SemaphoreType.DMA((2,)),
            pltpu.SemaphoreType.DMA((2,)),
            pltpu.SemaphoreType.DMA((2, ntr)),
            pltpu.SemaphoreType.DMA((2, ntr)),
            pltpu.SemaphoreType.DMA((ntr,)),
        ],
        compiler_params=pltpu.CompilerParams(
            collective_id=0, has_side_effects=True, vmem_limit_bytes=24 * 1024 * 1024
        ),
    )(jnp.swapaxes(tracers, 1, 2), jnp.swapaxes(ocean, 1, 2), expand_mask(wet_blocks), surface_light, rates)
    return jnp.swapaxes(outs[0], 1, 2), jnp.swapaxes(outs[1], 1, 2), jnp.swapaxes(outs[2], 0, 1)


def solution(mesh):
    return jax.shard_map(
        functools.partial(shards, mesh.shape["grp"], mesh.shape["tile"]),
        mesh=mesh,
        in_specs=(
            P(None, None, "grp", "tile"),
            P(None, None, "grp", "tile"),
            P("grp", "tile"),
            P("grp", "tile"),
            P(),
        ),
        out_specs=(
            P(None, None, "grp", "tile"),
            P(None, None, "grp", "tile"),
            P(None, "grp", "tile"),
        ),
        check_vma=False,
    )
```

```python
import functools

import jax
import jax.numpy as jnp
from jax import lax
from jax.experimental import pallas as pl
from jax.experimental.pallas import tpu as pltpu
from jax.sharding import PartitionSpec as P

WBY = 4
WBX = 16

time_step = 0.3
coriolis = 0.2
viscosity = 0.1
diffusion = 0.05
thermal = 0.2
haline = 0.15
gravity_red = 0.05
react_step = 0.5
water_atten = 0.3
chloro_atten = 0.2

MESH = pl.DeviceIdType.MESH
F32 = jnp.float32
BF16 = jnp.bfloat16
GROUP = 8
HALO = 4
RIM = [(0, 1), (0, 2), (1, 1), (1, 2), (1, 3), (2, 1), (2, 2), (3, 1), (3, 2)]
DIRS = [(dy, dx) for dy in (-1, 0, 1) for dx in (-1, 0, 1) if (dy, dx) != (0, 0)]


def minmod(a, b):
    return jnp.minimum(jnp.maximum(a, jnp.minimum(b, 0.0)), jnp.maximum(b, 0.0))


def lanes(x, shift):
    return pltpu.roll(x, shift % x.shape[1], 1)


def lane_of(shape):
    return lax.broadcasted_iota(jnp.int32, shape, 1)


def depth_sum(x):
    level = lax.broadcasted_iota(jnp.int32, x.shape, 0)
    step = 1
    while step < x.shape[0]:
        x = x + jnp.where(level >= step, pltpu.roll(x, step, 0), 0.0)
        step *= 2
    return x


def loop(steps, at_once, body):
    at_once = at_once if steps % at_once == 0 else 1

    def some(i, carry):
        for k in range(at_once):
            body(at_once * i + k)
        return carry

    if steps == at_once:
        some(0, 0)
    else:
        lax.fori_loop(0, steps // at_once, some, 0)


def split_speed(speed):
    return jnp.maximum(speed, 0.0), jnp.minimum(speed, 0.0)


def kernel(ngrp, ntile, ny, tr, oc, wet, light, rates, oc_out, tr_out, heat_out,
           halo_tr, halo_oc, send_oc, px, st, wind, oe, o1, m1, z1, m2, z2, ua, va, ub, vb, tt, plain, around,
           p_send, p_recv, o_send, o_recv, t_send, t_recv, f_send):
    ntr, cells, nx = tr.shape
    nz = cells // ny

    def spot(row, level=0, count=nz):
        return pl.ds(level * ny + row, count, stride=ny)

    gy, gx = lax.axis_index("grp"), lax.axis_index("tile")
    there = {-1: gy > 0, 0: True, 1: gy < ngrp - 1}
    over = {-1: gx > 0, 0: True, 1: gx < ntile - 1}

    def has(dy, dx):
        return jnp.logical_and(there[dy], over[dx])

    def peer(dy, dx):
        return (gy + dy, gx + dx)

    barrier = pltpu.get_barrier_semaphore()
    for dy, dx in DIRS:
        @pl.when(has(dy, dx))
        def _(dy=dy, dx=dx):
            pl.semaphore_signal(barrier, inc=1, device_id=peer(dy, dx), device_id_type=MESH)

    relay = ngrp % 4 == 0
    place = gy % 4
    partner = (jnp.where(place < 2, gy + 2, gy - 2), gx)
    if relay:
        pl.semaphore_signal(barrier, inc=1, device_id=partner, device_id_type=MESH)

    num_y = 1 + there[-1].astype(jnp.int32) + there[1].astype(jnp.int32)
    num_x = 1 + over[-1].astype(jnp.int32) + over[1].astype(jnp.int32)

    for field in range(4):
        for row in range(ny):
            oe[field, row + 3] = oc[field, spot(row), :]
    for slot, (field, depth) in enumerate(RIM):
        send_oc[1, slot] = oe[field, ny + 3 - depth].astype(BF16)
        send_oc[0, slot] = oe[field, depth + 2].astype(BF16)

    lane = lane_of((nz, nx))

    def unfold(t):
        plain[t] = tr[t].astype(F32)

    loop(ntr, 2, unfold)

    def pack(row):
        total = jnp.zeros((nz, nx), F32)
        for field in range(ntr + 4):
            x = plain[field, spot(row), :] if field < ntr else oe[field - ntr, row + 3]
            total = jnp.where(lane // GROUP == field, lanes(x, GROUP * field + GROUP // 2), total)
        px[1, row + 2] = total.astype(BF16)

    loop(ny, 1, pack)

    def edge_copy(dy, dx, index):
        rows = {-1: (2, ny + 2, 2), 0: (2, 2, ny), 1: (ny, 0, 2)}[dy]
        return pltpu.make_async_remote_copy(
            src_ref=px.at[1, pl.ds(rows[0], rows[2])], dst_ref=px.at[1 - dx, pl.ds(rows[1], rows[2])],
            send_sem=p_send.at[index], recv_sem=p_recv.at[index], device_id=peer(dy, dx), device_id_type=MESH)

    def ocean_copy(side):
        return pltpu.make_async_remote_copy(
            src_ref=send_oc.at[side], dst_ref=halo_oc.at[side],
            send_sem=o_send.at[side], recv_sem=o_recv.at[side],
            device_id=peer(2 * side - 1, 0), device_id_type=MESH)

    def tracer_copy(side, t):
        return pltpu.make_async_remote_copy(
            src_ref=tr.at[t], dst_ref=halo_tr.at[side, t],
            send_sem=t_send.at[side, t], recv_sem=t_recv.at[side, t],
            device_id=peer(2 * side - 1, 0), device_id_type=MESH)

    def forward_copy(side, t):
        return pltpu.make_async_remote_copy(
            src_ref=halo_tr.at[side, t], dst_ref=halo_tr.at[1 - side, t],
            send_sem=f_send.at[t], recv_sem=t_recv.at[1 - side, t], device_id=partner, device_id_type=MESH)

    def sends(side):
        direct = there[2 * side - 1]
        return jnp.logical_and(direct, place != 2 - side) if relay else direct

    def forwards(side):
        return place == 3 * side

    def forward(t):
        if relay:
            for side in (0, 1):
                @pl.when(forwards(side))
                def _(side=side):
                    tracer_copy(side, t).wait_recv()
                    forward_copy(side, t).start()

    pl.semaphore_wait(barrier, num_y * num_x - 1 + (1 if relay else 0))
    for index, (dy, dx) in enumerate(DIRS):
        @pl.when(has(dy, dx))
        def _(dy=dy, dx=dx, index=index):
            edge_copy(dy, dx, index).start()
    for side in (0, 1):
        @pl.when(there[2 * side - 1])
        def _(side=side):
            ocean_copy(side).start()
    for t in range(ntr):
        for side in (0, 1):
            @pl.when(sends(side))
            def _(side=side, t=t):
                tracer_copy(side, t).start()

    for index, (dy, dx) in enumerate(DIRS):
        @pl.when(jnp.logical_not(has(-dy, -dx)))
        def _(dy=dy, dx=dx):
            start, size = {-1: (ny + 2, 2), 0: (2, ny), 1: (0, 2)}[dy]
            px[1 - dx, pl.ds(start, size)] = jnp.zeros((size, nz, nx), BF16)
    for side in (0, 1):
        @pl.when(jnp.logical_not(there[1 - 2 * side]))
        def _(side=side):
            halo_oc[side] = jnp.zeros(halo_oc.shape[1:], BF16)
            halo_tr[side] = jnp.zeros(halo_tr.shape[1:], BF16)

    for index, (dy, dx) in enumerate(DIRS):
        @pl.when(has(-dy, -dx))
        def _(dy=dy, dx=dx, index=index):
            edge_copy(dy, dx, index).wait_recv()

    part = lane % GROUP
    near_west = part == GROUP // 2

    group = lane // GROUP
    source = lax.broadcasted_iota(jnp.int32, (nx, 2 * nx), 0)
    target = lax.broadcasted_iota(jnp.int32, (nx, 2 * nx), 1)
    spread = jnp.logical_and(source // GROUP == ntr + target // nx, source % GROUP == target % GROUP)
    spread = jnp.where(spread, 1.0, 0.0).astype(BF16)

    def strips(slot):
        west, own, east = (px[k, slot].astype(F32) for k in range(3))
        low = part < GROUP // 2
        left = jnp.where(low, west, own)
        right = jnp.where(low, own, east)
        st[0, slot], st[1, slot] = left, right
        for side, x in enumerate((left, right)):
            both = jnp.dot(x.astype(BF16), spread, preferred_element_type=F32)
            wind[side, 0, slot], wind[side, 1, slot] = both[:, :nx], both[:, nx:]
        mid = jnp.where(near_west, lanes(left, 1), lanes(right, -1))
        far = jnp.where(near_west, lanes(left, 2), lanes(right, -2))
        close = jnp.where(near_west, left, right)
        m1[slot] = mid
        z1[slot] = mid + 0.5 * minmod(mid - far, close - mid)

    loop(ny + 4, 4, strips)
    forward(0)

    blend = jnp.where(group < ntr + 2, viscosity, diffusion)

    def strip_step(side, slot):
        c = [st[side, slot + k] for k in (-2, -1, 0, 1, 2)]
        mid = c[2]
        zonal = wind[side, 0, slot]
        merid = [wind[side, 1, slot + k] for k in (-1, 0, 1)]
        east, west, north, south = lanes(mid, -1), lanes(mid, 1), c[3], c[1]
        gx_, gy_ = 0.5 * (east - west), 0.5 * (north - south)
        lap = east + west + north + south - 4.0 * mid
        force = jnp.where(group == ntr, thermal * lanes(gx_, -2 * GROUP) - haline * lanes(gx_, -3 * GROUP),
                          thermal * lanes(gy_, -GROUP) - haline * lanes(gy_, -2 * GROUP))
        press = gravity_red * depth_sum(force)
        rate = blend * lap - (zonal * gx_ + merid[1] * gy_)
        rate = rate + jnp.where(group == ntr, coriolis * merid[1] - press, 0.0)
        rate = rate - jnp.where(group == ntr + 1, coriolis * zonal + press, 0.0)
        ocean_one = mid + time_step * rate
        diff = mid - west
        half = 0.5 * minmod(diff, lanes(diff, -1))
        plus, minus = split_speed(0.5 * (zonal + lanes(zonal, 1)))
        flux = plus * lanes(mid + half, 1) + minus * (mid - half)
        div = lanes(flux, -1) - flux
        d = [c[k + 1] - c[k] for k in range(4)]
        h = [0.5 * minmod(d[k], d[k + 1]) for k in range(3)]
        fluxes = []
        for k in (0, 1):
            plus, minus = split_speed(0.5 * (merid[k] + merid[k + 1]))
            fluxes.append(plus * (c[k + 1] + h[k]) + minus * (c[k + 2] - h[k + 1]))
        div = div + (fluxes[1] - fluxes[0])
        tracer_one = (mid - time_step * div).astype(BF16).astype(F32)
        return jnp.where(group < ntr, tracer_one, ocean_one)

    in_west = jnp.where(over[-1], 1.0, 0.0)
    in_east = jnp.where(over[1], 1.0, 0.0)

    def strip_row(row):
        left = strip_step(0, row + 2)
        right = strip_step(1, row + 2)
        mid = jnp.where(near_west, in_west * lanes(left, 1), in_east * lanes(right, -1))
        far = jnp.where(near_west, in_west * lanes(left, 2), in_east * lanes(right, -2))
        close = jnp.where(near_west, left, right)
        m2[row] = mid
        z2[row] = mid + 0.5 * minmod(mid - far, close - mid)

    loop(ny, 4, strip_row)
    forward(1)

    for side in (0, 1):
        @pl.when(there[1 - 2 * side])
        def _(side=side):
            ocean_copy(side).wait_recv()
    for slot, (field, depth) in enumerate(RIM):
        oe[field, 3 - depth] = halo_oc[1, slot].astype(F32)
        oe[field, ny + 2 + depth] = halo_oc[0, slot].astype(F32)

    first, last = lane == 0, lane == nx - 1

    def shift_back(field):
        return -(GROUP * field + GROUP // 2)

    def ocean_rates(get, edge):
        center = [get(f, 0) for f in range(4)]
        zonal, merid = center[0], center[1]
        rates_, grads = [], []
        for f in range(4):
            mid = center[f]
            rim = lanes(edge, shift_back(ntr + f))
            east = jnp.where(last, rim, lanes(mid, -1))
            west = jnp.where(first, rim, lanes(mid, 1))
            north, south = get(f, 1), get(f, -1)
            gx_, gy_ = 0.5 * (east - west), 0.5 * (north - south)
            lap = east + west + north + south - 4.0 * mid
            rates_.append((viscosity if f < 2 else diffusion) * lap - (zonal * gx_ + merid * gy_))
            grads.append((gx_, gy_))
        px_, py_ = (gravity_red * depth_sum(thermal * grads[2][k] - haline * grads[3][k]) for k in (0, 1))
        rates_[0] = rates_[0] + coriolis * merid - px_
        rates_[1] = rates_[1] - coriolis * zonal - py_
        return rates_

    in_south = jnp.where(there[-1], 1.0, 0.0)
    in_north = jnp.where(there[1], 1.0, 0.0)

    def ocean_first(k):
        keep = jnp.where(k == 0, in_south, jnp.where(k == ny + 1, in_north, 1.0))
        rate = ocean_rates(lambda f, dy: oe[f, k + 2 + dy], m1[k + 1])
        for f in range(4):
            o1[f, k] = keep * (oe[f, k + 2] + time_step * rate[f])

    loop(ny + 2, 3, ocean_first)
    for t in (2, 3):
        forward(t)

    def ocean_second(row):
        rate = ocean_rates(lambda f, dy: o1[f, row + 1 + dy], m2[row])
        for f in range(4):
            oc_out[f, spot(row), :] = 0.5 * (oe[f, row + 3] + o1[f, row + 1] + time_step * rate[f])

    loop(ny, 4, ocean_second)
    forward(4)

    def zonal_faces(scale, mid, edge):
        rim = lanes(edge, shift_back(ntr))
        east = jnp.where(last, rim, lanes(mid, -1))
        west = jnp.where(first, rim, lanes(mid, 1))
        return split_speed(scale * (west + mid)) + split_speed(scale * (mid + east))

    def faces_first(j):
        for k, x in enumerate(zonal_faces(0.5 * time_step, oe[0, j + 1], m1[j])):
            ua[k, j] = x

    loop(ny + 4, 4, faces_first)

    def faces_second(j):
        for k, x in enumerate(zonal_faces(0.25 * time_step, o1[0, j + 1], m2[j])):
            ub[k, j] = x

    loop(ny, 4, faces_second)

    def merid_first(j):
        va[0, j], va[1, j] = split_speed((0.5 * time_step) * (oe[1, j] + oe[1, j + 1]))

    loop(ny + 5, 3, merid_first)

    def merid_second(j):
        vb[0, j], vb[1, j] = split_speed((0.25 * time_step) * (o1[1, j] + o1[1, j + 1]))

    loop(ny + 1, 5, merid_second)

    forward(5)
    ahead = 6
    chunk = 16
    clane = lane_of((chunk, nx))
    cfirst, clast = clane == 0, clane == nx - 1

    def zonal_part(c, rim, rim_value, speeds):
        diff = c - jnp.where(cfirst, rim, lanes(c, 1))
        ahead = jnp.where(clast, rim - c, lanes(diff, -1))
        half = 0.5 * minmod(diff, ahead)
        left, right = c + half, c - half
        before = jnp.where(cfirst, rim_value, lanes(left, 1))
        after = jnp.where(clast, rim_value, lanes(right, -1))
        return (speeds[2] * left + speeds[3] * after) - (speeds[0] * before + speeds[1] * right)

    def merid_part(c, speeds):
        d = [b - a for a, b in zip(c[:-1], c[1:])]
        h = [0.5 * minmod(a, b) for a, b in zip(d[:-1], d[1:])]
        flux = []
        for k in range(len(h) - 1):
            plus, minus = speeds(k)
            flux.append(plus * (c[k + 1] + h[k]) + minus * (c[k + 2] - h[k + 1]))
        return [b - a for a, b in zip(flux[:-1], flux[1:])]

    def tracer(t, carry):
        for side in (0, 1):
            arrives = there[1 - 2 * side]
            if relay:
                arrives = jnp.logical_and(arrives, jnp.logical_not(forwards(side)))

            @pl.when(arrives)
            def _(side=side):
                tracer_copy(side, t).wait_recv()
        for side in (0, 1):
            around[side] = halo_tr[side, t].astype(F32)
        back = nx - (GROUP * t + GROUP // 2)

        def levels(zc):
            zs = pl.ds(zc * chunk, chunk)
            c = [around[1, spot(k + ny - HALO, zc * chunk, chunk), :] for k in range(HALO)]
            c += [plain[t, spot(k, zc * chunk, chunk), :] for k in range(ny)]
            c += [around[0, spot(k, zc * chunk, chunk), :] for k in range(HALO)]
            along_y = merid_part(c, lambda k: (va[0, k, zs], va[1, k, zs]))
            one = []
            for j in range(ny + 4):
                rim = pltpu.roll(m1[j, zs], back, 1)
                rim_value = pltpu.roll(z1[j, zs], back, 1)
                mid = c[j + 2]
                div = zonal_part(mid, rim, rim_value, [ua[k, j, zs] for k in range(4)]) + along_y[j]
                new = (mid - div).astype(BF16).astype(F32)
                if j < 2:
                    new = in_south * new
                if j >= ny + 2:
                    new = in_north * new
                one.append(new)
            along_y = merid_part(one, lambda k: (vb[0, k, zs], vb[1, k, zs]))
            for j in range(ny):
                rim = pltpu.roll(m2[j, zs], back, 1)
                rim_value = pltpu.roll(z2[j, zs], back, 1)
                mid = one[j + 2]
                div = zonal_part(mid, rim, rim_value, [ub[k, j, zs] for k in range(4)]) + along_y[j]
                tt[t, j, zs] = 0.5 * (c[j + 4] + mid) - div

        for zc in range(nz // chunk):
            levels(zc)
        if relay:
            @pl.when(t + ahead < ntr)
            def _():
                forward(t + ahead)
        return carry

    lax.fori_loop(0, ntr, tracer, 0)

    def react(row):
        mask = react_step * wet[pl.ds(row, 1), :]

        for zc in range(nz // chunk):
            zs = pl.ds(zc * chunk, chunk)
            x = [tt[t, row, zs] for t in range(ntr)]
            for a in range(ntr):
                total = rates[a, 0] * x[0]
                for b in range(1, ntr):
                    total = total + rates[a, b] * x[b]
                reacted = x[a] + mask * total
                plain[a, spot(row, zc * chunk, chunk), :] = reacted
                if a == 0:
                    tt[0, row, zs] = water_atten + chloro_atten * reacted * reacted

    loop(ny, 1, react)

    def heat(row):
        att = tt[0, row]
        cum = depth_sum(att)
        heating = (wet[pl.ds(row, 1), :] * light[pl.ds(row, 1), :]) * (jnp.exp(att - cum) - jnp.exp(-cum))
        heat_out[spot(row), :] = heating
        oc_out[2, spot(row), :] = oc_out[2, spot(row), :] + time_step * heating

    loop(ny, 4, heat)

    def fold(t):
        tr_out[t] = plain[t].astype(BF16)

    loop(ntr, 2, fold)

    for index, (dy, dx) in enumerate(DIRS):
        @pl.when(has(dy, dx))
        def _(dy=dy, dx=dx, index=index):
            edge_copy(dy, dx, index).wait_send()
    for side in (0, 1):
        @pl.when(there[2 * side - 1])
        def _(side=side):
            ocean_copy(side).wait_send()

        @pl.when(sends(side))
        def _(side=side):
            for t in range(ntr):
                tracer_copy(side, t).wait_send()

        if relay:
            @pl.when(forwards(side))
            def _(side=side):
                for t in range(ntr):
                    forward_copy(side, t).wait_send()


def expand_mask(wet_blocks):
    blocks = wet_blocks.astype(F32)
    rows, cols = blocks.shape
    wide = jnp.broadcast_to(blocks[:, None, :, None], (rows, WBY, cols, WBX))
    return wide.reshape(rows * WBY, cols * WBX)


def shards(ngrp, ntile, ocean, tracers, wet_blocks, surface_light, rates):
    ntr, nz, ny, nx = tracers.shape
    vmem = pl.BlockSpec(memory_space=pltpu.VMEM)
    level, flat = (nz, nx), (nz * ny, nx)
    outs = pl.pallas_call(
        functools.partial(kernel, ngrp, ntile, ny),
        out_shape=(
            jax.ShapeDtypeStruct((4,) + flat, F32),
            jax.ShapeDtypeStruct((ntr,) + flat, BF16),
            jax.ShapeDtypeStruct(flat, F32),
        ),
        in_specs=[vmem] * 4 + [pl.BlockSpec(memory_space=pltpu.SMEM)],
        out_specs=(vmem,) * 3,
        scratch_shapes=[
            pltpu.VMEM((2, ntr) + flat, BF16),
            pltpu.VMEM((2, len(RIM)) + level, BF16),
            pltpu.VMEM((2, len(RIM)) + level, BF16),
            pltpu.VMEM((3, ny + 4) + level, BF16),
            pltpu.VMEM((2, ny + 4) + level, F32),
            pltpu.VMEM((2, 2, ny + 4) + level, F32),
            pltpu.VMEM((4, ny + 6) + level, F32),
            pltpu.VMEM((4, ny + 2) + level, F32),
            pltpu.VMEM((ny + 4,) + level, F32),
            pltpu.VMEM((ny + 4,) + level, F32),
            pltpu.VMEM((ny,) + level, F32),
            pltpu.VMEM((ny,) + level, F32),
            pltpu.VMEM((4, ny + 4) + level, F32),
            pltpu.VMEM((2, ny + 5) + level, F32),
            pltpu.VMEM((4, ny) + level, F32),
            pltpu.VMEM((2, ny + 1) + level, F32),
            pltpu.VMEM((ntr, ny) + level, F32),
            pltpu.VMEM((ntr,) + flat, F32),
            pltpu.VMEM((2,) + flat, F32),
            pltpu.SemaphoreType.DMA((len(DIRS),)),
            pltpu.SemaphoreType.DMA((len(DIRS),)),
            pltpu.SemaphoreType.DMA((2,)),
            pltpu.SemaphoreType.DMA((2,)),
            pltpu.SemaphoreType.DMA((2, ntr)),
            pltpu.SemaphoreType.DMA((2, ntr)),
            pltpu.SemaphoreType.DMA((ntr,)),
        ],
        compiler_params=pltpu.CompilerParams(
            collective_id=0, has_side_effects=True, vmem_limit_bytes=24 * 1024 * 1024
        ),
    )(tracers.reshape((ntr,) + flat), ocean.reshape((4,) + flat), expand_mask(wet_blocks), surface_light, rates)
    return outs[0].reshape(ocean.shape), outs[1].reshape(tracers.shape), outs[2].reshape(ocean.shape[1:])


def solution(mesh):
    return jax.shard_map(
        functools.partial(shards, mesh.shape["grp"], mesh.shape["tile"]),
        mesh=mesh,
        in_specs=(
            P(None, None, "grp", "tile"),
            P(None, None, "grp", "tile"),
            P("grp", "tile"),
            P("grp", "tile"),
            P(),
        ),
        out_specs=(
            P(None, None, "grp", "tile"),
            P(None, None, "grp", "tile"),
            P(None, "grp", "tile"),
        ),
        check_vma=False,
    )
```

```python
import functools

import jax
import jax.numpy as jnp
from jax import lax
from jax.experimental import pallas as pl
from jax.experimental.pallas import tpu as pltpu
from jax.sharding import PartitionSpec as P

WBY = 4
WBX = 16

time_step = 0.3
coriolis = 0.2
viscosity = 0.1
diffusion = 0.05
thermal = 0.2
haline = 0.15
gravity_red = 0.05
react_step = 0.5
water_atten = 0.3
chloro_atten = 0.2

VMEM_GRANT = 64000 * 1024
MESH = pl.DeviceIdType.MESH
F32 = jnp.float32
BF16 = jnp.bfloat16
GROUP = 8
HALO = 4
RIM = [(0, 1), (0, 2), (1, 1), (1, 2), (1, 3), (2, 1), (2, 2), (3, 1), (3, 2)]
DIRS = [(dy, dx) for dy in (-1, 0, 1) for dx in (-1, 0, 1) if (dy, dx) != (0, 0)]


def minmod(a, b):
    return jnp.minimum(jnp.maximum(a, jnp.minimum(b, 0.0)), jnp.maximum(b, 0.0))


def lanes(x, shift):
    return pltpu.roll(x, shift % x.shape[1], 1)


def lane_of(shape):
    return lax.broadcasted_iota(jnp.int32, shape, 1)


def depth_sum(x):
    level = lax.broadcasted_iota(jnp.int32, x.shape, 0)
    step = 1
    while step < x.shape[0]:
        x = x + jnp.where(level >= step, pltpu.roll(x, step, 0), 0.0)
        step *= 2
    return x


def loop(steps, at_once, body):
    at_once = at_once if steps % at_once == 0 else 1

    def some(i, carry):
        for k in range(at_once):
            body(at_once * i + k)
        return carry

    if steps == at_once:
        some(0, 0)
    else:
        lax.fori_loop(0, steps // at_once, some, 0)


def split_speed(speed):
    return jnp.maximum(speed, 0.0), jnp.minimum(speed, 0.0)


def kernel(ngrp, ntile, ny, tr_in, oc_in, wet_in, light_in, rates_in, oc_final, tr_final, heat_final,
           oc_out, tr_out, heat_out, out_sem, tr, oc, wet, light, rates, in_sem, halo_tr, halo_oc, send_oc, px, st, wind, oe, o1, m1, z1, m2, z2, ua, va, ub, vb, tt, plain, around,
           p_send, p_recv, o_send, o_recv, t_send, t_recv, f_send):
    ntr, cells, nx = tr.shape
    nz = cells // ny

    def spot(row, level=0, count=nz):
        return pl.ds(level * ny + row, count, stride=ny)

    gy, gx = lax.axis_index("grp"), lax.axis_index("tile")
    inputs = [pltpu.make_async_copy(src, dst, in_sem.at[k]) for k, (src, dst) in enumerate(
        [(oc_in, oc), (tr_in, tr), (wet_in, wet), (light_in, light), (rates_in, rates)])]
    for copy in inputs:
        copy.start()
    there = {-1: gy > 0, 0: True, 1: gy < ngrp - 1}
    over = {-1: gx > 0, 0: True, 1: gx < ntile - 1}

    def has(dy, dx):
        return jnp.logical_and(there[dy], over[dx])

    def peer(dy, dx):
        return (gy + dy, gx + dx)

    barrier = pltpu.get_barrier_semaphore()
    for dy, dx in DIRS:
        @pl.when(has(dy, dx))
        def _(dy=dy, dx=dx):
            pl.semaphore_signal(barrier, inc=1, device_id=peer(dy, dx), device_id_type=MESH)

    relay = ngrp % 4 == 0
    place = gy % 4
    partner = (jnp.where(place < 2, gy + 2, gy - 2), gx)
    if relay:
        pl.semaphore_signal(barrier, inc=1, device_id=partner, device_id_type=MESH)

    num_y = 1 + there[-1].astype(jnp.int32) + there[1].astype(jnp.int32)
    num_x = 1 + over[-1].astype(jnp.int32) + over[1].astype(jnp.int32)

    inputs[0].wait()
    for field in range(4):
        for row in range(ny):
            oe[field, row + 3] = oc[field, spot(row), :]
    for slot, (field, depth) in enumerate(RIM):
        send_oc[1, slot] = oe[field, ny + 3 - depth].astype(BF16)
        send_oc[0, slot] = oe[field, depth + 2].astype(BF16)

    lane = lane_of((nz, nx))

    inputs[1].wait()

    def unfold(t):
        plain[t] = tr[t].astype(F32)

    loop(ntr, 2, unfold)

    def pack(row):
        total = jnp.zeros((nz, nx), F32)
        for field in range(ntr + 4):
            x = plain[field, spot(row), :] if field < ntr else oe[field - ntr, row + 3]
            total = jnp.where(lane // GROUP == field, lanes(x, GROUP * field + GROUP // 2), total)
        px[1, row + 2] = total.astype(BF16)

    loop(ny, 1, pack)

    def edge_copy(dy, dx, index):
        rows = {-1: (2, ny + 2, 2), 0: (2, 2, ny), 1: (ny, 0, 2)}[dy]
        return pltpu.make_async_remote_copy(
            src_ref=px.at[1, pl.ds(rows[0], rows[2])], dst_ref=px.at[1 - dx, pl.ds(rows[1], rows[2])],
            send_sem=p_send.at[index], recv_sem=p_recv.at[index], device_id=peer(dy, dx), device_id_type=MESH)

    def ocean_copy(side):
        return pltpu.make_async_remote_copy(
            src_ref=send_oc.at[side], dst_ref=halo_oc.at[side],
            send_sem=o_send.at[side], recv_sem=o_recv.at[side],
            device_id=peer(2 * side - 1, 0), device_id_type=MESH)

    def tracer_copy(side, t):
        return pltpu.make_async_remote_copy(
            src_ref=tr.at[t], dst_ref=halo_tr.at[side, t],
            send_sem=t_send.at[side, t], recv_sem=t_recv.at[side, t],
            device_id=peer(2 * side - 1, 0), device_id_type=MESH)

    def forward_copy(side, t):
        return pltpu.make_async_remote_copy(
            src_ref=halo_tr.at[side, t], dst_ref=halo_tr.at[1 - side, t],
            send_sem=f_send.at[t], recv_sem=t_recv.at[1 - side, t], device_id=partner, device_id_type=MESH)

    def sends(side):
        direct = there[2 * side - 1]
        return jnp.logical_and(direct, place != 2 - side) if relay else direct

    def forwards(side):
        return place == 3 * side

    def forward(t):
        if relay:
            for side in (0, 1):
                @pl.when(forwards(side))
                def _(side=side):
                    tracer_copy(side, t).wait_recv()
                    forward_copy(side, t).start()

    pl.semaphore_wait(barrier, num_y * num_x - 1 + (1 if relay else 0))
    for index, (dy, dx) in enumerate(DIRS):
        @pl.when(has(dy, dx))
        def _(dy=dy, dx=dx, index=index):
            edge_copy(dy, dx, index).start()
    for side in (0, 1):
        @pl.when(there[2 * side - 1])
        def _(side=side):
            ocean_copy(side).start()
    for t in range(ntr):
        for side in (0, 1):
            @pl.when(sends(side))
            def _(side=side, t=t):
                tracer_copy(side, t).start()

    for index, (dy, dx) in enumerate(DIRS):
        @pl.when(jnp.logical_not(has(-dy, -dx)))
        def _(dy=dy, dx=dx):
            start, size = {-1: (ny + 2, 2), 0: (2, ny), 1: (0, 2)}[dy]
            px[1 - dx, pl.ds(start, size)] = jnp.zeros((size, nz, nx), BF16)
    for side in (0, 1):
        @pl.when(jnp.logical_not(there[1 - 2 * side]))
        def _(side=side):
            halo_oc[side] = jnp.zeros(halo_oc.shape[1:], BF16)
            halo_tr[side] = jnp.zeros(halo_tr.shape[1:], BF16)

    for index, (dy, dx) in enumerate(DIRS):
        @pl.when(has(-dy, -dx))
        def _(dy=dy, dx=dx, index=index):
            edge_copy(dy, dx, index).wait_recv()

    part = lane % GROUP
    near_west = part == GROUP // 2

    group = lane // GROUP
    source = lax.broadcasted_iota(jnp.int32, (nx, 2 * nx), 0)
    target = lax.broadcasted_iota(jnp.int32, (nx, 2 * nx), 1)
    spread = jnp.logical_and(source // GROUP == ntr + target // nx, source % GROUP == target % GROUP)
    spread = jnp.where(spread, 1.0, 0.0).astype(BF16)

    def strips(slot):
        west, own, east = (px[k, slot].astype(F32) for k in range(3))
        low = part < GROUP // 2
        left = jnp.where(low, west, own)
        right = jnp.where(low, own, east)
        st[0, slot], st[1, slot] = left, right
        for side, x in enumerate((left, right)):
            both = jnp.dot(x.astype(BF16), spread, preferred_element_type=F32)
            wind[side, 0, slot], wind[side, 1, slot] = both[:, :nx], both[:, nx:]
        mid = jnp.where(near_west, lanes(left, 1), lanes(right, -1))
        far = jnp.where(near_west, lanes(left, 2), lanes(right, -2))
        close = jnp.where(near_west, left, right)
        m1[slot] = mid
        z1[slot] = mid + 0.5 * minmod(mid - far, close - mid)

    loop(ny + 4, 4, strips)
    forward(0)

    blend = jnp.where(group < ntr + 2, viscosity, diffusion)

    def strip_step(side, slot):
        c = [st[side, slot + k] for k in (-2, -1, 0, 1, 2)]
        mid = c[2]
        zonal = wind[side, 0, slot]
        merid = [wind[side, 1, slot + k] for k in (-1, 0, 1)]
        east, west, north, south = lanes(mid, -1), lanes(mid, 1), c[3], c[1]
        gx_, gy_ = 0.5 * (east - west), 0.5 * (north - south)
        lap = east + west + north + south - 4.0 * mid
        force = jnp.where(group == ntr, thermal * lanes(gx_, -2 * GROUP) - haline * lanes(gx_, -3 * GROUP),
                          thermal * lanes(gy_, -GROUP) - haline * lanes(gy_, -2 * GROUP))
        press = gravity_red * depth_sum(force)
        rate = blend * lap - (zonal * gx_ + merid[1] * gy_)
        rate = rate + jnp.where(group == ntr, coriolis * merid[1] - press, 0.0)
        rate = rate - jnp.where(group == ntr + 1, coriolis * zonal + press, 0.0)
        ocean_one = mid + time_step * rate
        diff = mid - west
        half = 0.5 * minmod(diff, lanes(diff, -1))
        plus, minus = split_speed(0.5 * (zonal + lanes(zonal, 1)))
        flux = plus * lanes(mid + half, 1) + minus * (mid - half)
        div = lanes(flux, -1) - flux
        d = [c[k + 1] - c[k] for k in range(4)]
        h = [0.5 * minmod(d[k], d[k + 1]) for k in range(3)]
        fluxes = []
        for k in (0, 1):
            plus, minus = split_speed(0.5 * (merid[k] + merid[k + 1]))
            fluxes.append(plus * (c[k + 1] + h[k]) + minus * (c[k + 2] - h[k + 1]))
        div = div + (fluxes[1] - fluxes[0])
        tracer_one = (mid - time_step * div).astype(BF16).astype(F32)
        return jnp.where(group < ntr, tracer_one, ocean_one)

    in_west = jnp.where(over[-1], 1.0, 0.0)
    in_east = jnp.where(over[1], 1.0, 0.0)

    def strip_row(row):
        left = strip_step(0, row + 2)
        right = strip_step(1, row + 2)
        mid = jnp.where(near_west, in_west * lanes(left, 1), in_east * lanes(right, -1))
        far = jnp.where(near_west, in_west * lanes(left, 2), in_east * lanes(right, -2))
        close = jnp.where(near_west, left, right)
        m2[row] = mid
        z2[row] = mid + 0.5 * minmod(mid - far, close - mid)

    loop(ny, 4, strip_row)
    for t in (1, 2):
        forward(t)

    for side in (0, 1):
        @pl.when(there[1 - 2 * side])
        def _(side=side):
            ocean_copy(side).wait_recv()
    for slot, (field, depth) in enumerate(RIM):
        oe[field, 3 - depth] = halo_oc[1, slot].astype(F32)
        oe[field, ny + 2 + depth] = halo_oc[0, slot].astype(F32)

    first, last = lane == 0, lane == nx - 1

    def shift_back(field):
        return -(GROUP * field + GROUP // 2)

    def ocean_rates(get, edge):
        center = [get(f, 0) for f in range(4)]
        zonal, merid = center[0], center[1]
        rates_, grads = [], []
        for f in range(4):
            mid = center[f]
            rim = lanes(edge, shift_back(ntr + f))
            east = jnp.where(last, rim, lanes(mid, -1))
            west = jnp.where(first, rim, lanes(mid, 1))
            north, south = get(f, 1), get(f, -1)
            gx_, gy_ = 0.5 * (east - west), 0.5 * (north - south)
            lap = east + west + north + south - 4.0 * mid
            rates_.append((viscosity if f < 2 else diffusion) * lap - (zonal * gx_ + merid * gy_))
            grads.append((gx_, gy_))
        px_, py_ = (gravity_red * depth_sum(thermal * grads[2][k] - haline * grads[3][k]) for k in (0, 1))
        rates_[0] = rates_[0] + coriolis * merid - px_
        rates_[1] = rates_[1] - coriolis * zonal - py_
        return rates_

    in_south = jnp.where(there[-1], 1.0, 0.0)
    in_north = jnp.where(there[1], 1.0, 0.0)

    def ocean_first(k):
        keep = jnp.where(k == 0, in_south, jnp.where(k == ny + 1, in_north, 1.0))
        rate = ocean_rates(lambda f, dy: oe[f, k + 2 + dy], m1[k + 1])
        for f in range(4):
            o1[f, k] = keep * (oe[f, k + 2] + time_step * rate[f])

    loop(ny + 2, 3, ocean_first)
    for t in (3, 4):
        forward(t)

    def ocean_second(row):
        rate = ocean_rates(lambda f, dy: o1[f, row + 1 + dy], m2[row])
        for f in range(4):
            oc_out[f, spot(row), :] = 0.5 * (oe[f, row + 3] + o1[f, row + 1] + time_step * rate[f])

    loop(ny, 4, ocean_second)
    results = [pltpu.make_async_copy(oc_out.at[f], oc_final.at[f], out_sem.at[f]) for f in range(4)]
    results.append(pltpu.make_async_copy(tr_out, tr_final, out_sem.at[4]))
    results.append(pltpu.make_async_copy(heat_out, heat_final, out_sem.at[5]))
    for f in (0, 1, 3):
        results[f].start()
    forward(5)

    def zonal_faces(scale, mid, edge):
        rim = lanes(edge, shift_back(ntr))
        east = jnp.where(last, rim, lanes(mid, -1))
        west = jnp.where(first, rim, lanes(mid, 1))
        return split_speed(scale * (west + mid)) + split_speed(scale * (mid + east))

    def faces_first(j):
        for k, x in enumerate(zonal_faces(0.5 * time_step, oe[0, j + 1], m1[j])):
            ua[k, j] = x

    loop(ny + 4, 4, faces_first)

    def faces_second(j):
        for k, x in enumerate(zonal_faces(0.25 * time_step, o1[0, j + 1], m2[j])):
            ub[k, j] = x

    loop(ny, 4, faces_second)

    def merid_first(j):
        va[0, j], va[1, j] = split_speed((0.5 * time_step) * (oe[1, j] + oe[1, j + 1]))

    loop(ny + 5, 3, merid_first)

    def merid_second(j):
        vb[0, j], vb[1, j] = split_speed((0.25 * time_step) * (o1[1, j] + o1[1, j + 1]))

    loop(ny + 1, 5, merid_second)

    forward(6)
    ahead = 7
    chunk = 16
    clane = lane_of((chunk, nx))
    cfirst, clast = clane == 0, clane == nx - 1

    def zonal_part(c, rim, rim_value, speeds):
        diff = c - jnp.where(cfirst, rim, lanes(c, 1))
        ahead = jnp.where(clast, rim - c, lanes(diff, -1))
        half = 0.5 * minmod(diff, ahead)
        left, right = c + half, c - half
        before = jnp.where(cfirst, rim_value, lanes(left, 1))
        after = jnp.where(clast, rim_value, lanes(right, -1))
        return (speeds[2] * left + speeds[3] * after) - (speeds[0] * before + speeds[1] * right)

    def merid_part(c, speeds):
        d = [b - a for a, b in zip(c[:-1], c[1:])]
        h = [0.5 * minmod(a, b) for a, b in zip(d[:-1], d[1:])]
        flux = []
        for k in range(len(h) - 1):
            plus, minus = speeds(k)
            flux.append(plus * (c[k + 1] + h[k]) + minus * (c[k + 2] - h[k + 1]))
        return [b - a for a, b in zip(flux[:-1], flux[1:])]

    def tracer(t, carry):
        for side in (0, 1):
            arrives = there[1 - 2 * side]
            if relay:
                arrives = jnp.logical_and(arrives, jnp.logical_not(forwards(side)))

            @pl.when(arrives)
            def _(side=side):
                tracer_copy(side, t).wait_recv()
        for side in (0, 1):
            around[side] = halo_tr[side, t].astype(F32)
        back = nx - (GROUP * t + GROUP // 2)

        def levels(zc):
            zs = pl.ds(zc * chunk, chunk)
            c = [around[1, spot(k + ny - HALO, zc * chunk, chunk), :] for k in range(HALO)]
            c += [plain[t, spot(k, zc * chunk, chunk), :] for k in range(ny)]
            c += [around[0, spot(k, zc * chunk, chunk), :] for k in range(HALO)]
            along_y = merid_part(c, lambda k: (va[0, k, zs], va[1, k, zs]))
            one = []
            for j in range(ny + 4):
                rim = pltpu.roll(m1[j, zs], back, 1)
                rim_value = pltpu.roll(z1[j, zs], back, 1)
                mid = c[j + 2]
                div = zonal_part(mid, rim, rim_value, [ua[k, j, zs] for k in range(4)]) + along_y[j]
                new = (mid - div).astype(BF16).astype(F32)
                if j < 2:
                    new = in_south * new
                if j >= ny + 2:
                    new = in_north * new
                one.append(new)
            along_y = merid_part(one, lambda k: (vb[0, k, zs], vb[1, k, zs]))
            for j in range(ny):
                rim = pltpu.roll(m2[j, zs], back, 1)
                rim_value = pltpu.roll(z2[j, zs], back, 1)
                mid = one[j + 2]
                div = zonal_part(mid, rim, rim_value, [ub[k, j, zs] for k in range(4)]) + along_y[j]
                tt[t, j, zs] = 0.5 * (c[j + 4] + mid) - div

        for zc in range(nz // chunk):
            levels(zc)
        if relay:
            @pl.when(t + ahead < ntr)
            def _():
                forward(t + ahead)
        return carry

    lax.fori_loop(0, ntr, tracer, 0)

    for copy in inputs[2:]:
        copy.wait()
    block = lane_of((1, nx)) // WBX

    def wet_row(row):
        total = jnp.zeros((1, nx), F32)
        for k in range(nx // WBX):
            total = jnp.where(block == k, wet[row // WBY, k].astype(F32), total)
        return total

    def react(row):
        mask = react_step * wet_row(row)

        for zc in range(nz // chunk):
            zs = pl.ds(zc * chunk, chunk)
            x = [tt[t, row, zs] for t in range(ntr)]
            for a in range(ntr):
                total = rates[a, 0] * x[0]
                for b in range(1, ntr):
                    total = total + rates[a, b] * x[b]
                reacted = x[a] + mask * total
                plain[a, spot(row, zc * chunk, chunk), :] = reacted
                if a == 0:
                    tt[0, row, zs] = water_atten + chloro_atten * reacted * reacted

    loop(ny, 2, react)

    def fold(t):
        tr_out[t] = plain[t].astype(BF16)

    loop(ntr, 2, fold)
    results[4].start()

    def heat(row):
        att = tt[0, row]
        cum = depth_sum(att)
        heating = (wet_row(row) * light[pl.ds(row, 1), :]) * (jnp.exp(att - cum) - jnp.exp(-cum))
        heat_out[spot(row), :] = heating
        oc_out[2, spot(row), :] = oc_out[2, spot(row), :] + time_step * heating

    loop(ny, 4, heat)
    results[2].start()
    results[5].start()

    for index, (dy, dx) in enumerate(DIRS):
        @pl.when(has(dy, dx))
        def _(dy=dy, dx=dx, index=index):
            edge_copy(dy, dx, index).wait_send()
    for side in (0, 1):
        @pl.when(there[2 * side - 1])
        def _(side=side):
            ocean_copy(side).wait_send()

        @pl.when(sends(side))
        def _(side=side):
            for t in range(ntr):
                tracer_copy(side, t).wait_send()

        if relay:
            @pl.when(forwards(side))
            def _(side=side):
                for t in range(ntr):
                    forward_copy(side, t).wait_send()
    for copy in results:
        copy.wait()


def hand_out(*refs):
    count = len(refs) // 2
    copies = [pltpu.make_async_copy(refs[k], refs[count + k], refs[-1].at[k]) for k in range(count)]
    for copy in copies:
        copy.start()
    for copy in copies:
        copy.wait()


def shards(ngrp, ntile, ocean, tracers, wet_blocks, surface_light, rates):
    ntr, nz, ny, nx = tracers.shape
    hbm = pl.BlockSpec(memory_space=pltpu.HBM)
    level, flat = (nz, nx), (nz * ny, nx)
    outs = pl.pallas_call(
        functools.partial(kernel, ngrp, ntile, ny),
        out_shape=(
            jax.ShapeDtypeStruct((4,) + flat, F32),
            jax.ShapeDtypeStruct((ntr,) + flat, BF16),
            jax.ShapeDtypeStruct(flat, F32),
        ),
        in_specs=[hbm] * 5,
        out_specs=(hbm,) * 3,
        scratch_shapes=[
            pltpu.VMEM((4,) + flat, F32),
            pltpu.VMEM((ntr,) + flat, BF16),
            pltpu.VMEM(flat, F32),
            pltpu.SemaphoreType.DMA((6,)),
            pltpu.VMEM((ntr,) + flat, BF16),
            pltpu.VMEM((4,) + flat, F32),
            pltpu.SMEM(wet_blocks.shape, jnp.int32),
            pltpu.VMEM(surface_light.shape, F32),
            pltpu.SMEM(rates.shape, F32),
            pltpu.SemaphoreType.DMA((5,)),
            pltpu.VMEM((2, ntr) + flat, BF16),
            pltpu.VMEM((2, len(RIM)) + level, BF16),
            pltpu.VMEM((2, len(RIM)) + level, BF16),
            pltpu.VMEM((3, ny + 4) + level, BF16),
            pltpu.VMEM((2, ny + 4) + level, F32),
            pltpu.VMEM((2, 2, ny + 4) + level, F32),
            pltpu.VMEM((4, ny + 6) + level, F32),
            pltpu.VMEM((4, ny + 2) + level, F32),
            pltpu.VMEM((ny + 4,) + level, F32),
            pltpu.VMEM((ny + 4,) + level, F32),
            pltpu.VMEM((ny,) + level, F32),
            pltpu.VMEM((ny,) + level, F32),
            pltpu.VMEM((4, ny + 4) + level, F32),
            pltpu.VMEM((2, ny + 5) + level, F32),
            pltpu.VMEM((4, ny) + level, F32),
            pltpu.VMEM((2, ny + 1) + level, F32),
            pltpu.VMEM((ntr, ny) + level, F32),
            pltpu.VMEM((ntr,) + flat, F32),
            pltpu.VMEM((2,) + flat, F32),
            pltpu.SemaphoreType.DMA((len(DIRS),)),
            pltpu.SemaphoreType.DMA((len(DIRS),)),
            pltpu.SemaphoreType.DMA((2,)),
            pltpu.SemaphoreType.DMA((2,)),
            pltpu.SemaphoreType.DMA((2, ntr)),
            pltpu.SemaphoreType.DMA((2, ntr)),
            pltpu.SemaphoreType.DMA((ntr,)),
        ],
        compiler_params=pltpu.CompilerParams(
            collective_id=0, has_side_effects=True, vmem_limit_bytes=VMEM_GRANT
        ),
    )(tracers.reshape((ntr,) + flat), ocean.reshape((4,) + flat), wet_blocks, surface_light, rates)
    outs = pl.pallas_call(
        hand_out,
        out_shape=[jax.ShapeDtypeStruct(out.shape, out.dtype) for out in outs],
        in_specs=[hbm] * 3,
        out_specs=[hbm] * 3,
        scratch_shapes=[pltpu.SemaphoreType.DMA((3,))],
        compiler_params=pltpu.CompilerParams(vmem_limit_bytes=VMEM_GRANT),
    )(*outs)
    return outs[0].reshape(ocean.shape), outs[1].reshape(tracers.shape), outs[2].reshape(ocean.shape[1:])


def solution(mesh):
    return jax.shard_map(
        functools.partial(shards, mesh.shape["grp"], mesh.shape["tile"]),
        mesh=mesh,
        in_specs=(
            P(None, None, "grp", "tile"),
            P(None, None, "grp", "tile"),
            P("grp", "tile"),
            P("grp", "tile"),
            P(),
        ),
        out_specs=(
            P(None, None, "grp", "tile"),
            P(None, None, "grp", "tile"),
            P(None, "grp", "tile"),
        ),
        check_vma=False,
    )
```

```python
import functools

import jax
import jax.numpy as jnp
from jax import lax
from jax.experimental import pallas as pl
from jax.experimental.pallas import tpu as pltpu
from jax.sharding import PartitionSpec as P

WBY = 4
WBX = 16

time_step = 0.3
coriolis = 0.2
viscosity = 0.1
diffusion = 0.05
thermal = 0.2
haline = 0.15
gravity_red = 0.05
react_step = 0.5
water_atten = 0.3
chloro_atten = 0.2

VMEM_GRANT = 64000 * 1024
MESH = pl.DeviceIdType.MESH
F32 = jnp.float32
BF16 = jnp.bfloat16
GROUP = 8
HALO = 4
RIM = [(0, 1), (0, 2), (1, 1), (1, 2), (1, 3), (2, 1), (2, 2), (3, 1), (3, 2)]
DIRS = [(dy, dx) for dy in (-1, 0, 1) for dx in (-1, 0, 1) if (dy, dx) != (0, 0)]


def minmod(a, b):
    return jnp.minimum(jnp.maximum(a, jnp.minimum(b, 0.0)), jnp.maximum(b, 0.0))


def lanes(x, shift):
    return pltpu.roll(x, shift % x.shape[1], 1)


def lane_of(shape):
    return lax.broadcasted_iota(jnp.int32, shape, 1)


def depth_sum(x):
    level = lax.broadcasted_iota(jnp.int32, x.shape, 0)
    step = 1
    while step < x.shape[0]:
        x = x + jnp.where(level >= step, pltpu.roll(x, step, 0), 0.0)
        step *= 2
    return x


def loop(steps, at_once, body):
    at_once = at_once if steps % at_once == 0 else 1

    def some(i, carry):
        for k in range(at_once):
            body(at_once * i + k)
        return carry

    if steps == at_once:
        some(0, 0)
    else:
        lax.fori_loop(0, steps // at_once, some, 0)


def split_speed(speed):
    return jnp.maximum(speed, 0.0), jnp.minimum(speed, 0.0)


def kernel(ngrp, ntile, ny, tr_in, oc_in, wet_in, light_in, rates_in, oc_final, tr_final, heat_final,
           oc_out, tr_out, heat_out, out_sem, tr, oc, wet, light, rates, in_sem, halo_tr, halo_oc, send_oc, px, st, wind, oe, o1, m1, z1, m2, z2, ua, va, ub, vb, tt, plain, around,
           p_send, p_recv, o_send, o_recv, t_send, t_recv, f_send):
    ntr, cells, nx = tr.shape
    nz = cells // ny

    def spot(row, level=0, count=nz):
        return pl.ds(level * ny + row, count, stride=ny)

    gy, gx = lax.axis_index("grp"), lax.axis_index("tile")
    inputs = [pltpu.make_async_copy(src, dst, in_sem.at[k]) for k, (src, dst) in enumerate(
        [(oc_in, oc), (tr_in, tr), (wet_in, wet), (light_in, light), (rates_in, rates)])]
    for copy in inputs:
        copy.start()
    there = {-1: gy > 0, 0: True, 1: gy < ngrp - 1}
    over = {-1: gx > 0, 0: True, 1: gx < ntile - 1}

    def has(dy, dx):
        return jnp.logical_and(there[dy], over[dx])

    def peer(dy, dx):
        return (gy + dy, gx + dx)

    barrier = pltpu.get_barrier_semaphore()
    for dy, dx in DIRS:
        @pl.when(has(dy, dx))
        def _(dy=dy, dx=dx):
            pl.semaphore_signal(barrier, inc=1, device_id=peer(dy, dx), device_id_type=MESH)

    relay = ngrp % 4 == 0
    place = gy % 4
    partner = (jnp.where(place < 2, gy + 2, gy - 2), gx)
    if relay:
        pl.semaphore_signal(barrier, inc=1, device_id=partner, device_id_type=MESH)

    num_y = 1 + there[-1].astype(jnp.int32) + there[1].astype(jnp.int32)
    num_x = 1 + over[-1].astype(jnp.int32) + over[1].astype(jnp.int32)

    inputs[0].wait()
    for field in range(4):
        for row in range(ny):
            oe[field, row + 3] = oc[field, spot(row), :]
    for slot, (field, depth) in enumerate(RIM):
        send_oc[1, slot] = oe[field, ny + 3 - depth].astype(BF16)
        send_oc[0, slot] = oe[field, depth + 2].astype(BF16)

    lane = lane_of((nz, nx))

    inputs[1].wait()

    def unfold(t):
        plain[t] = tr[t].astype(F32)

    loop(ntr, 2, unfold)

    def pack(row):
        total = jnp.zeros((nz, nx), F32)
        for field in range(ntr + 4):
            x = plain[field, spot(row), :] if field < ntr else oe[field - ntr, row + 3]
            total = jnp.where(lane // GROUP == field, lanes(x, GROUP * field + GROUP // 2), total)
        px[1, row + 2] = total.astype(BF16)

    loop(ny, 1, pack)

    def edge_copy(dy, dx, index):
        rows = {-1: (2, ny + 2, 2), 0: (2, 2, ny), 1: (ny, 0, 2)}[dy]
        return pltpu.make_async_remote_copy(
            src_ref=px.at[1, pl.ds(rows[0], rows[2])], dst_ref=px.at[1 - dx, pl.ds(rows[1], rows[2])],
            send_sem=p_send.at[index], recv_sem=p_recv.at[index], device_id=peer(dy, dx), device_id_type=MESH)

    def ocean_copy(side):
        return pltpu.make_async_remote_copy(
            src_ref=send_oc.at[side], dst_ref=halo_oc.at[side],
            send_sem=o_send.at[side], recv_sem=o_recv.at[side],
            device_id=peer(2 * side - 1, 0), device_id_type=MESH)

    def tracer_copy(side, t):
        return pltpu.make_async_remote_copy(
            src_ref=tr.at[t], dst_ref=halo_tr.at[side, t],
            send_sem=t_send.at[side, t], recv_sem=t_recv.at[side, t],
            device_id=peer(2 * side - 1, 0), device_id_type=MESH)

    def forward_copy(side, t):
        return pltpu.make_async_remote_copy(
            src_ref=halo_tr.at[side, t], dst_ref=halo_tr.at[1 - side, t],
            send_sem=f_send.at[t], recv_sem=t_recv.at[1 - side, t], device_id=partner, device_id_type=MESH)

    def sends(side):
        direct = there[2 * side - 1]
        return jnp.logical_and(direct, place != 2 - side) if relay else direct

    def forwards(side):
        return place == 3 * side

    def forward(t):
        if relay:
            for side in (0, 1):
                @pl.when(forwards(side))
                def _(side=side):
                    tracer_copy(side, t).wait_recv()
                    forward_copy(side, t).start()

    pl.semaphore_wait(barrier, num_y * num_x - 1 + (1 if relay else 0))
    for index, (dy, dx) in enumerate(DIRS):
        @pl.when(has(dy, dx))
        def _(dy=dy, dx=dx, index=index):
            edge_copy(dy, dx, index).start()
    for side in (0, 1):
        @pl.when(there[2 * side - 1])
        def _(side=side):
            ocean_copy(side).start()
    def launch(t):
        for side in (0, 1):
            @pl.when(sends(side))
            def _(side=side):
                tracer_copy(side, t).start()

    in_flight = min(3, ntr)
    pumped = min(7, ntr - in_flight)

    def pump(t):
        if t < pumped:
            for side in (0, 1):
                @pl.when(sends(side))
                def _(side=side):
                    tracer_copy(side, t).wait_send()
            launch(t + in_flight)

    for t in range(in_flight):
        launch(t)

    for index, (dy, dx) in enumerate(DIRS):
        @pl.when(jnp.logical_not(has(-dy, -dx)))
        def _(dy=dy, dx=dx):
            start, size = {-1: (ny + 2, 2), 0: (2, ny), 1: (0, 2)}[dy]
            px[1 - dx, pl.ds(start, size)] = jnp.zeros((size, nz, nx), BF16)
    for side in (0, 1):
        @pl.when(jnp.logical_not(there[1 - 2 * side]))
        def _(side=side):
            halo_oc[side] = jnp.zeros(halo_oc.shape[1:], BF16)
            halo_tr[side] = jnp.zeros(halo_tr.shape[1:], BF16)

    for index, (dy, dx) in enumerate(DIRS):
        @pl.when(has(-dy, -dx))
        def _(dy=dy, dx=dx, index=index):
            edge_copy(dy, dx, index).wait_recv()
    pump(0)

    part = lane % GROUP
    near_west = part == GROUP // 2

    group = lane // GROUP
    source = lax.broadcasted_iota(jnp.int32, (nx, 2 * nx), 0)
    target = lax.broadcasted_iota(jnp.int32, (nx, 2 * nx), 1)
    spread = jnp.logical_and(source // GROUP == ntr + target // nx, source % GROUP == target % GROUP)
    spread = jnp.where(spread, 1.0, 0.0).astype(BF16)

    def strips(slot):
        west, own, east = (px[k, slot].astype(F32) for k in range(3))
        low = part < GROUP // 2
        left = jnp.where(low, west, own)
        right = jnp.where(low, own, east)
        st[0, slot], st[1, slot] = left, right
        for side, x in enumerate((left, right)):
            both = jnp.dot(x.astype(BF16), spread, preferred_element_type=F32)
            wind[side, 0, slot], wind[side, 1, slot] = both[:, :nx], both[:, nx:]
        mid = jnp.where(near_west, lanes(left, 1), lanes(right, -1))
        far = jnp.where(near_west, lanes(left, 2), lanes(right, -2))
        close = jnp.where(near_west, left, right)
        m1[slot] = mid
        z1[slot] = mid + 0.5 * minmod(mid - far, close - mid)

    loop(ny + 4, 4, strips)
    pump(1)
    forward(0)

    blend = jnp.where(group < ntr + 2, viscosity, diffusion)

    def strip_step(side, slot):
        c = [st[side, slot + k] for k in (-2, -1, 0, 1, 2)]
        mid = c[2]
        zonal = wind[side, 0, slot]
        merid = [wind[side, 1, slot + k] for k in (-1, 0, 1)]
        east, west, north, south = lanes(mid, -1), lanes(mid, 1), c[3], c[1]
        gx_, gy_ = 0.5 * (east - west), 0.5 * (north - south)
        lap = east + west + north + south - 4.0 * mid
        force = jnp.where(group == ntr, thermal * lanes(gx_, -2 * GROUP) - haline * lanes(gx_, -3 * GROUP),
                          thermal * lanes(gy_, -GROUP) - haline * lanes(gy_, -2 * GROUP))
        press = gravity_red * depth_sum(force)
        rate = blend * lap - (zonal * gx_ + merid[1] * gy_)
        rate = rate + jnp.where(group == ntr, coriolis * merid[1] - press, 0.0)
        rate = rate - jnp.where(group == ntr + 1, coriolis * zonal + press, 0.0)
        ocean_one = mid + time_step * rate
        diff = mid - west
        half = 0.5 * minmod(diff, lanes(diff, -1))
        plus, minus = split_speed(0.5 * (zonal + lanes(zonal, 1)))
        flux = plus * lanes(mid + half, 1) + minus * (mid - half)
        div = lanes(flux, -1) - flux
        d = [c[k + 1] - c[k] for k in range(4)]
        h = [0.5 * minmod(d[k], d[k + 1]) for k in range(3)]
        fluxes = []
        for k in (0, 1):
            plus, minus = split_speed(0.5 * (merid[k] + merid[k + 1]))
            fluxes.append(plus * (c[k + 1] + h[k]) + minus * (c[k + 2] - h[k + 1]))
        div = div + (fluxes[1] - fluxes[0])
        tracer_one = (mid - time_step * div).astype(BF16).astype(F32)
        return jnp.where(group < ntr, tracer_one, ocean_one)

    in_west = jnp.where(over[-1], 1.0, 0.0)
    in_east = jnp.where(over[1], 1.0, 0.0)

    def strip_row(row):
        left = strip_step(0, row + 2)
        right = strip_step(1, row + 2)
        mid = jnp.where(near_west, in_west * lanes(left, 1), in_east * lanes(right, -1))
        far = jnp.where(near_west, in_west * lanes(left, 2), in_east * lanes(right, -2))
        close = jnp.where(near_west, left, right)
        m2[row] = mid
        z2[row] = mid + 0.5 * minmod(mid - far, close - mid)

    loop(ny, 4, strip_row)
    pump(2)
    forward(1)
    pump(3)

    for side in (0, 1):
        @pl.when(there[1 - 2 * side])
        def _(side=side):
            ocean_copy(side).wait_recv()
    for slot, (field, depth) in enumerate(RIM):
        oe[field, 3 - depth] = halo_oc[1, slot].astype(F32)
        oe[field, ny + 2 + depth] = halo_oc[0, slot].astype(F32)

    first, last = lane == 0, lane == nx - 1

    def shift_back(field):
        return -(GROUP * field + GROUP // 2)

    def ocean_rates(get, edge):
        center = [get(f, 0) for f in range(4)]
        zonal, merid = center[0], center[1]
        rates_, grads = [], []
        for f in range(4):
            mid = center[f]
            rim = lanes(edge, shift_back(ntr + f))
            east = jnp.where(last, rim, lanes(mid, -1))
            west = jnp.where(first, rim, lanes(mid, 1))
            north, south = get(f, 1), get(f, -1)
            gx_, gy_ = 0.5 * (east - west), 0.5 * (north - south)
            lap = east + west + north + south - 4.0 * mid
            rates_.append((viscosity if f < 2 else diffusion) * lap - (zonal * gx_ + merid * gy_))
            grads.append((gx_, gy_))
        px_, py_ = (gravity_red * depth_sum(thermal * grads[2][k] - haline * grads[3][k]) for k in (0, 1))
        rates_[0] = rates_[0] + coriolis * merid - px_
        rates_[1] = rates_[1] - coriolis * zonal - py_
        return rates_

    in_south = jnp.where(there[-1], 1.0, 0.0)
    in_north = jnp.where(there[1], 1.0, 0.0)

    def ocean_first(k):
        keep = jnp.where(k == 0, in_south, jnp.where(k == ny + 1, in_north, 1.0))
        rate = ocean_rates(lambda f, dy: oe[f, k + 2 + dy], m1[k + 1])
        for f in range(4):
            o1[f, k] = keep * (oe[f, k + 2] + time_step * rate[f])

    loop(ny + 2, 3, ocean_first)
    pump(4)
    for t in (2, 3):
        forward(t)

    def ocean_second(row):
        rate = ocean_rates(lambda f, dy: o1[f, row + 1 + dy], m2[row])
        for f in range(4):
            oc_out[f, spot(row), :] = 0.5 * (oe[f, row + 3] + o1[f, row + 1] + time_step * rate[f])

    loop(ny, 4, ocean_second)
    results = [pltpu.make_async_copy(oc_out.at[f], oc_final.at[f], out_sem.at[f]) for f in range(4)]
    results.append(pltpu.make_async_copy(tr_out, tr_final, out_sem.at[4]))
    results.append(pltpu.make_async_copy(heat_out, heat_final, out_sem.at[5]))
    for f in (0, 1, 3):
        results[f].start()
    pump(5)
    forward(4)

    def zonal_faces(scale, mid, edge):
        rim = lanes(edge, shift_back(ntr))
        east = jnp.where(last, rim, lanes(mid, -1))
        west = jnp.where(first, rim, lanes(mid, 1))
        return split_speed(scale * (west + mid)) + split_speed(scale * (mid + east))

    def faces_first(j):
        for k, x in enumerate(zonal_faces(0.5 * time_step, oe[0, j + 1], m1[j])):
            ua[k, j] = x

    loop(ny + 4, 4, faces_first)

    def faces_second(j):
        for k, x in enumerate(zonal_faces(0.25 * time_step, o1[0, j + 1], m2[j])):
            ub[k, j] = x

    loop(ny, 4, faces_second)

    def merid_first(j):
        va[0, j], va[1, j] = split_speed((0.5 * time_step) * (oe[1, j] + oe[1, j + 1]))

    loop(ny + 5, 3, merid_first)

    def merid_second(j):
        vb[0, j], vb[1, j] = split_speed((0.25 * time_step) * (o1[1, j] + o1[1, j + 1]))

    loop(ny + 1, 5, merid_second)

    pump(6)
    forward(5)
    ahead = 6
    chunk = 16
    clane = lane_of((chunk, nx))
    cfirst, clast = clane == 0, clane == nx - 1

    def zonal_part(c, rim, rim_value, speeds):
        diff = c - jnp.where(cfirst, rim, lanes(c, 1))
        ahead = jnp.where(clast, rim - c, lanes(diff, -1))
        half = 0.5 * minmod(diff, ahead)
        left, right = c + half, c - half
        before = jnp.where(cfirst, rim_value, lanes(left, 1))
        after = jnp.where(clast, rim_value, lanes(right, -1))
        return (speeds[2] * left + speeds[3] * after) - (speeds[0] * before + speeds[1] * right)

    def merid_part(c, speeds):
        d = [b - a for a, b in zip(c[:-1], c[1:])]
        h = [0.5 * minmod(a, b) for a, b in zip(d[:-1], d[1:])]
        flux = []
        for k in range(len(h) - 1):
            plus, minus = speeds(k)
            flux.append(plus * (c[k + 1] + h[k]) + minus * (c[k + 2] - h[k + 1]))
        return [b - a for a, b in zip(flux[:-1], flux[1:])]

    def tracer(t, carry):
        for side in (0, 1):
            arrives = there[1 - 2 * side]
            if relay:
                arrives = jnp.logical_and(arrives, jnp.logical_not(forwards(side)))

            @pl.when(arrives)
            def _(side=side):
                tracer_copy(side, t).wait_recv()
        for side in (0, 1):
            around[side] = halo_tr[side, t].astype(F32)
        back = nx - (GROUP * t + GROUP // 2)

        def levels(zc):
            zs = pl.ds(zc * chunk, chunk)
            c = [around[1, spot(k + ny - HALO, zc * chunk, chunk), :] for k in range(HALO)]
            c += [plain[t, spot(k, zc * chunk, chunk), :] for k in range(ny)]
            c += [around[0, spot(k, zc * chunk, chunk), :] for k in range(HALO)]
            along_y = merid_part(c, lambda k: (va[0, k, zs], va[1, k, zs]))
            one = []
            for j in range(ny + 4):
                rim = pltpu.roll(m1[j, zs], back, 1)
                rim_value = pltpu.roll(z1[j, zs], back, 1)
                mid = c[j + 2]
                div = zonal_part(mid, rim, rim_value, [ua[k, j, zs] for k in range(4)]) + along_y[j]
                new = (mid - div).astype(BF16).astype(F32)
                if j < 2:
                    new = in_south * new
                if j >= ny + 2:
                    new = in_north * new
                one.append(new)
            along_y = merid_part(one, lambda k: (vb[0, k, zs], vb[1, k, zs]))
            for j in range(ny):
                rim = pltpu.roll(m2[j, zs], back, 1)
                rim_value = pltpu.roll(z2[j, zs], back, 1)
                mid = one[j + 2]
                div = zonal_part(mid, rim, rim_value, [ub[k, j, zs] for k in range(4)]) + along_y[j]
                tt[t, j, zs] = 0.5 * (c[j + 4] + mid) - div

        for zc in range(nz // chunk):
            levels(zc)
        if relay:
            @pl.when(t + ahead < ntr)
            def _():
                forward(t + ahead)
        return carry

    lax.fori_loop(0, ntr, tracer, 0)

    for copy in inputs[2:]:
        copy.wait()
    block = lane_of((1, nx)) // WBX

    def wet_row(row):
        total = jnp.zeros((1, nx), F32)
        for k in range(nx // WBX):
            total = jnp.where(block == k, wet[row // WBY, k].astype(F32), total)
        return total

    def react(row):
        mask = react_step * wet_row(row)

        for zc in range(nz // chunk):
            zs = pl.ds(zc * chunk, chunk)
            x = [tt[t, row, zs] for t in range(ntr)]
            for a in range(ntr):
                total = rates[a, 0] * x[0]
                for b in range(1, ntr):
                    total = total + rates[a, b] * x[b]
                reacted = x[a] + mask * total
                plain[a, spot(row, zc * chunk, chunk), :] = reacted
                if a == 0:
                    tt[0, row, zs] = water_atten + chloro_atten * reacted * reacted

    loop(ny, 2, react)

    def fold(t):
        tr_out[t] = plain[t].astype(BF16)

    loop(ntr, 2, fold)
    results[4].start()

    def heat(row):
        att = tt[0, row]
        cum = depth_sum(att)
        heating = (wet_row(row) * light[pl.ds(row, 1), :]) * (jnp.exp(att - cum) - jnp.exp(-cum))
        heat_out[spot(row), :] = heating
        oc_out[2, spot(row), :] = oc_out[2, spot(row), :] + time_step * heating

    loop(ny, 4, heat)
    results[2].start()
    results[5].start()

    for index, (dy, dx) in enumerate(DIRS):
        @pl.when(has(dy, dx))
        def _(dy=dy, dx=dx, index=index):
            edge_copy(dy, dx, index).wait_send()
    for side in (0, 1):
        @pl.when(there[2 * side - 1])
        def _(side=side):
            ocean_copy(side).wait_send()

        @pl.when(sends(side))
        def _(side=side):
            for t in range(pumped, ntr):
                tracer_copy(side, t).wait_send()

        if relay:
            @pl.when(forwards(side))
            def _(side=side):
                for t in range(ntr):
                    forward_copy(side, t).wait_send()
    for copy in results:
        copy.wait()


def hand_out(ocean, tracers, heat, ocean_out, tracers_out, heat_out, ocean_held, tracers_held, heat_held, in_sem, out_sem):
    pieces = [(ocean.at[f], ocean_held.at[f], ocean_out.at[f]) for f in range(ocean.shape[0])]
    pieces += [(heat, heat_held, heat_out)]
    half = tracers.shape[0] // 2
    for part in (pl.ds(0, half), pl.ds(half, tracers.shape[0] - half)):
        pieces.append((tracers.at[part], tracers_held.at[part], tracers_out.at[part]))
    loads = [pltpu.make_async_copy(p[0], p[1], in_sem.at[k]) for k, p in enumerate(pieces)]
    stores = [pltpu.make_async_copy(p[1], p[2], out_sem.at[k]) for k, p in enumerate(pieces)]
    for copy in loads:
        copy.start()
    for load, store in zip(loads, stores):
        load.wait()
        store.start()
    for copy in stores:
        copy.wait()


def shards(ngrp, ntile, ocean, tracers, wet_blocks, surface_light, rates):
    ntr, nz, ny, nx = tracers.shape
    hbm = pl.BlockSpec(memory_space=pltpu.HBM)
    level, flat = (nz, nx), (nz * ny, nx)
    outs = pl.pallas_call(
        functools.partial(kernel, ngrp, ntile, ny),
        out_shape=(
            jax.ShapeDtypeStruct((4,) + flat, F32),
            jax.ShapeDtypeStruct((ntr,) + flat, BF16),
            jax.ShapeDtypeStruct(flat, F32),
        ),
        in_specs=[hbm] * 5,
        out_specs=(hbm,) * 3,
        scratch_shapes=[
            pltpu.VMEM((4,) + flat, F32),
            pltpu.VMEM((ntr,) + flat, BF16),
            pltpu.VMEM(flat, F32),
            pltpu.SemaphoreType.DMA((6,)),
            pltpu.VMEM((ntr,) + flat, BF16),
            pltpu.VMEM((4,) + flat, F32),
            pltpu.SMEM(wet_blocks.shape, jnp.int32),
            pltpu.VMEM(surface_light.shape, F32),
            pltpu.SMEM(rates.shape, F32),
            pltpu.SemaphoreType.DMA((5,)),
            pltpu.VMEM((2, ntr) + flat, BF16),
            pltpu.VMEM((2, len(RIM)) + level, BF16),
            pltpu.VMEM((2, len(RIM)) + level, BF16),
            pltpu.VMEM((3, ny + 4) + level, BF16),
            pltpu.VMEM((2, ny + 4) + level, F32),
            pltpu.VMEM((2, 2, ny + 4) + level, F32),
            pltpu.VMEM((4, ny + 6) + level, F32),
            pltpu.VMEM((4, ny + 2) + level, F32),
            pltpu.VMEM((ny + 4,) + level, F32),
            pltpu.VMEM((ny + 4,) + level, F32),
            pltpu.VMEM((ny,) + level, F32),
            pltpu.VMEM((ny,) + level, F32),
            pltpu.VMEM((4, ny + 4) + level, F32),
            pltpu.VMEM((2, ny + 5) + level, F32),
            pltpu.VMEM((4, ny) + level, F32),
            pltpu.VMEM((2, ny + 1) + level, F32),
            pltpu.VMEM((ntr, ny) + level, F32),
            pltpu.VMEM((ntr,) + flat, F32),
            pltpu.VMEM((2,) + flat, F32),
            pltpu.SemaphoreType.DMA((len(DIRS),)),
            pltpu.SemaphoreType.DMA((len(DIRS),)),
            pltpu.SemaphoreType.DMA((2,)),
            pltpu.SemaphoreType.DMA((2,)),
            pltpu.SemaphoreType.DMA((2, ntr)),
            pltpu.SemaphoreType.DMA((2, ntr)),
            pltpu.SemaphoreType.DMA((ntr,)),
        ],
        compiler_params=pltpu.CompilerParams(
            collective_id=0, has_side_effects=True, vmem_limit_bytes=VMEM_GRANT
        ),
    )(tracers.reshape((ntr,) + flat), ocean.reshape((4,) + flat), wet_blocks, surface_light, rates)
    outs = pl.pallas_call(
        hand_out,
        out_shape=[jax.ShapeDtypeStruct(out.shape, out.dtype) for out in outs],
        in_specs=[hbm] * 3,
        out_specs=[hbm] * 3,
        scratch_shapes=[pltpu.VMEM(out.shape, out.dtype) for out in outs] + [pltpu.SemaphoreType.DMA((7,))] * 2,
        compiler_params=pltpu.CompilerParams(vmem_limit_bytes=VMEM_GRANT),
    )(*outs)
    return outs[0].reshape(ocean.shape), outs[1].reshape(tracers.shape), outs[2].reshape(ocean.shape[1:])


def solution(mesh):
    return jax.shard_map(
        functools.partial(shards, mesh.shape["grp"], mesh.shape["tile"]),
        mesh=mesh,
        in_specs=(
            P(None, None, "grp", "tile"),
            P(None, None, "grp", "tile"),
            P("grp", "tile"),
            P("grp", "tile"),
            P(),
        ),
        out_specs=(
            P(None, None, "grp", "tile"),
            P(None, None, "grp", "tile"),
            P(None, "grp", "tile"),
        ),
        check_vma=False,
    )
```

```python
import functools

import jax
import jax.numpy as jnp
from jax import lax
from jax.experimental import pallas as pl
from jax.experimental.pallas import tpu as pltpu
from jax.sharding import PartitionSpec as P

WBY = 4
WBX = 16

time_step = 0.3
coriolis = 0.2
viscosity = 0.1
diffusion = 0.05
thermal = 0.2
haline = 0.15
gravity_red = 0.05
react_step = 0.5
water_atten = 0.3
chloro_atten = 0.2

VMEM_GRANT = 64000 * 1024
MESH = pl.DeviceIdType.MESH
F32 = jnp.float32
BF16 = jnp.bfloat16
GROUP = 8
HALO = 4
RIM = [(0, 1), (0, 2), (1, 1), (1, 2), (1, 3), (2, 1), (2, 2), (3, 1), (3, 2)]
DIRS = [(dy, dx) for dy in (-1, 0, 1) for dx in (-1, 0, 1) if (dy, dx) != (0, 0)]


def minmod(a, b):
    return jnp.minimum(jnp.maximum(a, jnp.minimum(b, 0.0)), jnp.maximum(b, 0.0))


def lanes(x, shift):
    return pltpu.roll(x, shift % x.shape[1], 1)


def lane_of(shape):
    return lax.broadcasted_iota(jnp.int32, shape, 1)


def depth_sum(x):
    level = lax.broadcasted_iota(jnp.int32, x.shape, 0)
    step = 1
    while step < x.shape[0]:
        x = x + jnp.where(level >= step, pltpu.roll(x, step, 0), 0.0)
        step *= 2
    return x


def loop(steps, at_once, body):
    at_once = at_once if steps % at_once == 0 else 1

    def some(i, carry):
        for k in range(at_once):
            body(at_once * i + k)
        return carry

    if steps == at_once:
        some(0, 0)
    else:
        lax.fori_loop(0, steps // at_once, some, 0)


def split_speed(speed):
    return jnp.maximum(speed, 0.0), jnp.minimum(speed, 0.0)


def kernel(ngrp, ntile, ny, tr_in, oc_in, wet_in, light_in, rates_in, oc_final, tr_final, heat_final,
           oc_out, tr_out, heat_out, out_sem, tr, oc, wet, light, rates, in_sem, halo_tr, halo_oc, send_oc, px, st, wind, oe, o1, m1, z1, m2, z2, ua, va, ub, vb, tt, plain, around,
           p_send, p_recv, o_send, o_recv, t_send, t_recv, f_send):
    ntr, cells, nx = tr.shape
    nz = cells // ny

    def spot(row, level=0, count=nz):
        return pl.ds(level * ny + row, count, stride=ny)

    gy, gx = lax.axis_index("grp"), lax.axis_index("tile")
    inputs = [pltpu.make_async_copy(src, dst, in_sem.at[k]) for k, (src, dst) in enumerate(
        [(oc_in, oc), (tr_in, tr), (wet_in, wet), (light_in, light), (rates_in, rates)])]
    for copy in inputs:
        copy.start()
    there = {-1: gy > 0, 0: True, 1: gy < ngrp - 1}
    over = {-1: gx > 0, 0: True, 1: gx < ntile - 1}

    def has(dy, dx):
        return jnp.logical_and(there[dy], over[dx])

    def peer(dy, dx):
        return (gy + dy, gx + dx)

    barrier = pltpu.get_barrier_semaphore()
    for dy, dx in DIRS:
        @pl.when(has(dy, dx))
        def _(dy=dy, dx=dx):
            pl.semaphore_signal(barrier, inc=1, device_id=peer(dy, dx), device_id_type=MESH)

    relay = ngrp % 4 == 0
    place = gy % 4
    partner = (jnp.where(place < 2, gy + 2, gy - 2), gx)
    if relay:
        pl.semaphore_signal(barrier, inc=1, device_id=partner, device_id_type=MESH)

    num_y = 1 + there[-1].astype(jnp.int32) + there[1].astype(jnp.int32)
    num_x = 1 + over[-1].astype(jnp.int32) + over[1].astype(jnp.int32)

    inputs[0].wait()
    for field in range(4):
        for row in range(ny):
            oe[field, row + 3] = oc[field, spot(row), :]
    for slot, (field, depth) in enumerate(RIM):
        send_oc[1, slot] = oe[field, ny + 3 - depth].astype(BF16)
        send_oc[0, slot] = oe[field, depth + 2].astype(BF16)

    lane = lane_of((nz, nx))

    inputs[1].wait()

    def unfold(t):
        plain[t] = tr[t].astype(F32)

    loop(ntr, 2, unfold)

    def pack(row):
        total = jnp.zeros((nz, nx), F32)
        for field in range(ntr + 4):
            x = plain[field, spot(row), :] if field < ntr else oe[field - ntr, row + 3]
            total = jnp.where(lane // GROUP == field, lanes(x, GROUP * field + GROUP // 2), total)
        px[1, row + 2] = total.astype(BF16)

    loop(ny, 1, pack)

    def edge_copy(dy, dx, index):
        rows = {-1: (2, ny + 2, 2), 0: (2, 2, ny), 1: (ny, 0, 2)}[dy]
        return pltpu.make_async_remote_copy(
            src_ref=px.at[1, pl.ds(rows[0], rows[2])], dst_ref=px.at[1 - dx, pl.ds(rows[1], rows[2])],
            send_sem=p_send.at[index], recv_sem=p_recv.at[index], device_id=peer(dy, dx), device_id_type=MESH)

    def ocean_copy(side):
        return pltpu.make_async_remote_copy(
            src_ref=send_oc.at[side], dst_ref=halo_oc.at[side],
            send_sem=o_send.at[side], recv_sem=o_recv.at[side],
            device_id=peer(2 * side - 1, 0), device_id_type=MESH)

    def tracer_copy(side, t):
        return pltpu.make_async_remote_copy(
            src_ref=tr.at[t], dst_ref=halo_tr.at[side, t],
            send_sem=t_send.at[side, t], recv_sem=t_recv.at[side, t],
            device_id=peer(2 * side - 1, 0), device_id_type=MESH)

    def forward_copy(side, t):
        return pltpu.make_async_remote_copy(
            src_ref=halo_tr.at[side, t], dst_ref=halo_tr.at[1 - side, t],
            send_sem=f_send.at[t], recv_sem=t_recv.at[1 - side, t], device_id=partner, device_id_type=MESH)

    def sends(side):
        direct = there[2 * side - 1]
        return jnp.logical_and(direct, place != 2 - side) if relay else direct

    def forwards(side):
        return place == 3 * side

    def forward(t):
        if relay:
            for side in (0, 1):
                @pl.when(forwards(side))
                def _(side=side):
                    tracer_copy(side, t).wait_recv()
                    forward_copy(side, t).start()

    pl.semaphore_wait(barrier, num_y * num_x - 1 + (1 if relay else 0))
    for index, (dy, dx) in enumerate(DIRS):
        @pl.when(has(dy, dx))
        def _(dy=dy, dx=dx, index=index):
            edge_copy(dy, dx, index).start()
    for side in (0, 1):
        @pl.when(there[2 * side - 1])
        def _(side=side):
            ocean_copy(side).start()
    def launch(t):
        for side in (0, 1):
            @pl.when(sends(side))
            def _(side=side):
                tracer_copy(side, t).start()

    in_flight = min(3, ntr)
    pumped = min(7, ntr - in_flight)

    def pump(t):
        if t < pumped:
            for side in (0, 1):
                @pl.when(sends(side))
                def _(side=side):
                    tracer_copy(side, t).wait_send()
            launch(t + in_flight)

    for t in range(in_flight):
        launch(t)

    for index, (dy, dx) in enumerate(DIRS):
        @pl.when(jnp.logical_not(has(-dy, -dx)))
        def _(dy=dy, dx=dx):
            start, size = {-1: (ny + 2, 2), 0: (2, ny), 1: (0, 2)}[dy]
            px[1 - dx, pl.ds(start, size)] = jnp.zeros((size, nz, nx), BF16)
    for side in (0, 1):
        @pl.when(jnp.logical_not(there[1 - 2 * side]))
        def _(side=side):
            halo_oc[side] = jnp.zeros(halo_oc.shape[1:], BF16)
            halo_tr[side] = jnp.zeros(halo_tr.shape[1:], BF16)

    for index, (dy, dx) in enumerate(DIRS):
        @pl.when(has(-dy, -dx))
        def _(dy=dy, dx=dx, index=index):
            edge_copy(dy, dx, index).wait_recv()
    pump(0)

    part = lane % GROUP
    near_west = part == GROUP // 2

    group = lane // GROUP
    source = lax.broadcasted_iota(jnp.int32, (nx, 2 * nx), 0)
    target = lax.broadcasted_iota(jnp.int32, (nx, 2 * nx), 1)
    spread = jnp.logical_and(source // GROUP == ntr + target // nx, source % GROUP == target % GROUP)
    spread = jnp.where(spread, 1.0, 0.0).astype(BF16)

    def strips(slot):
        west, own, east = (px[k, slot].astype(F32) for k in range(3))
        low = part < GROUP // 2
        left = jnp.where(low, west, own)
        right = jnp.where(low, own, east)
        st[0, slot], st[1, slot] = left, right
        for side, x in enumerate((left, right)):
            both = jnp.dot(x.astype(BF16), spread, preferred_element_type=F32)
            wind[side, 0, slot], wind[side, 1, slot] = both[:, :nx], both[:, nx:]
        mid = jnp.where(near_west, lanes(left, 1), lanes(right, -1))
        far = jnp.where(near_west, lanes(left, 2), lanes(right, -2))
        close = jnp.where(near_west, left, right)
        m1[slot] = mid
        z1[slot] = mid + 0.5 * minmod(mid - far, close - mid)

    loop(ny + 4, 4, strips)
    pump(1)
    forward(0)

    blend = jnp.where(group < ntr + 2, viscosity, diffusion)

    def strip_step(side, slot):
        c = [st[side, slot + k] for k in (-2, -1, 0, 1, 2)]
        mid = c[2]
        zonal = wind[side, 0, slot]
        merid = [wind[side, 1, slot + k] for k in (-1, 0, 1)]
        east, west, north, south = lanes(mid, -1), lanes(mid, 1), c[3], c[1]
        gx_, gy_ = 0.5 * (east - west), 0.5 * (north - south)
        lap = east + west + north + south - 4.0 * mid
        force = jnp.where(group == ntr, thermal * lanes(gx_, -2 * GROUP) - haline * lanes(gx_, -3 * GROUP),
                          thermal * lanes(gy_, -GROUP) - haline * lanes(gy_, -2 * GROUP))
        press = gravity_red * depth_sum(force)
        rate = blend * lap - (zonal * gx_ + merid[1] * gy_)
        rate = rate + jnp.where(group == ntr, coriolis * merid[1] - press, 0.0)
        rate = rate - jnp.where(group == ntr + 1, coriolis * zonal + press, 0.0)
        ocean_one = mid + time_step * rate
        diff = mid - west
        half = 0.5 * minmod(diff, lanes(diff, -1))
        plus, minus = split_speed(0.5 * (zonal + lanes(zonal, 1)))
        flux = plus * lanes(mid + half, 1) + minus * (mid - half)
        div = lanes(flux, -1) - flux
        d = [c[k + 1] - c[k] for k in range(4)]
        h = [0.5 * minmod(d[k], d[k + 1]) for k in range(3)]
        fluxes = []
        for k in (0, 1):
            plus, minus = split_speed(0.5 * (merid[k] + merid[k + 1]))
            fluxes.append(plus * (c[k + 1] + h[k]) + minus * (c[k + 2] - h[k + 1]))
        div = div + (fluxes[1] - fluxes[0])
        tracer_one = (mid - time_step * div).astype(BF16).astype(F32)
        return jnp.where(group < ntr, tracer_one, ocean_one)

    in_west = jnp.where(over[-1], 1.0, 0.0)
    in_east = jnp.where(over[1], 1.0, 0.0)

    def strip_row(row):
        left = strip_step(0, row + 2)
        right = strip_step(1, row + 2)
        mid = jnp.where(near_west, in_west * lanes(left, 1), in_east * lanes(right, -1))
        far = jnp.where(near_west, in_west * lanes(left, 2), in_east * lanes(right, -2))
        close = jnp.where(near_west, left, right)
        m2[row] = mid
        z2[row] = mid + 0.5 * minmod(mid - far, close - mid)

    loop(ny, 4, strip_row)
    pump(2)
    forward(1)
    pump(3)

    for side in (0, 1):
        @pl.when(there[1 - 2 * side])
        def _(side=side):
            ocean_copy(side).wait_recv()
    for slot, (field, depth) in enumerate(RIM):
        oe[field, 3 - depth] = halo_oc[1, slot].astype(F32)
        oe[field, ny + 2 + depth] = halo_oc[0, slot].astype(F32)

    first, last = lane == 0, lane == nx - 1

    def shift_back(field):
        return -(GROUP * field + GROUP // 2)

    def ocean_rates(get, edge):
        center = [get(f, 0) for f in range(4)]
        zonal, merid = center[0], center[1]
        rates_, grads = [], []
        for f in range(4):
            mid = center[f]
            rim = lanes(edge, shift_back(ntr + f))
            east = jnp.where(last, rim, lanes(mid, -1))
            west = jnp.where(first, rim, lanes(mid, 1))
            north, south = get(f, 1), get(f, -1)
            gx_, gy_ = 0.5 * (east - west), 0.5 * (north - south)
            lap = east + west + north + south - 4.0 * mid
            rates_.append((viscosity if f < 2 else diffusion) * lap - (zonal * gx_ + merid * gy_))
            grads.append((gx_, gy_))
        px_, py_ = (gravity_red * depth_sum(thermal * grads[2][k] - haline * grads[3][k]) for k in (0, 1))
        rates_[0] = rates_[0] + coriolis * merid - px_
        rates_[1] = rates_[1] - coriolis * zonal - py_
        return rates_

    in_south = jnp.where(there[-1], 1.0, 0.0)
    in_north = jnp.where(there[1], 1.0, 0.0)

    def ocean_first(k):
        keep = jnp.where(k == 0, in_south, jnp.where(k == ny + 1, in_north, 1.0))
        rate = ocean_rates(lambda f, dy: oe[f, k + 2 + dy], m1[k + 1])
        for f in range(4):
            o1[f, k] = keep * (oe[f, k + 2] + time_step * rate[f])

    loop(ny + 2, 3, ocean_first)
    pump(4)
    for t in (2, 3):
        forward(t)

    def ocean_second(row):
        rate = ocean_rates(lambda f, dy: o1[f, row + 1 + dy], m2[row])
        for f in range(4):
            oc_out[f, spot(row), :] = 0.5 * (oe[f, row + 3] + o1[f, row + 1] + time_step * rate[f])

    loop(ny, 4, ocean_second)
    results = [pltpu.make_async_copy(oc_out.at[f], oc_final.at[f], out_sem.at[f]) for f in range(4)]
    results.append(pltpu.make_async_copy(tr_out, tr_final, out_sem.at[4]))
    results.append(pltpu.make_async_copy(heat_out, heat_final, out_sem.at[5]))
    for f in (0, 1, 3):
        results[f].start()
    pump(5)
    forward(4)

    def zonal_faces(scale, mid, edge):
        rim = lanes(edge, shift_back(ntr))
        east = jnp.where(last, rim, lanes(mid, -1))
        west = jnp.where(first, rim, lanes(mid, 1))
        return split_speed(scale * (west + mid)) + split_speed(scale * (mid + east))

    def faces_first(j):
        for k, x in enumerate(zonal_faces(0.5 * time_step, oe[0, j + 1], m1[j])):
            ua[k, j] = x

    loop(ny + 4, 4, faces_first)

    def faces_second(j):
        for k, x in enumerate(zonal_faces(0.25 * time_step, o1[0, j + 1], m2[j])):
            ub[k, j] = x

    loop(ny, 4, faces_second)

    def merid_first(j):
        va[0, j], va[1, j] = split_speed((0.5 * time_step) * (oe[1, j] + oe[1, j + 1]))

    loop(ny + 5, 3, merid_first)

    def merid_second(j):
        vb[0, j], vb[1, j] = split_speed((0.25 * time_step) * (o1[1, j] + o1[1, j + 1]))

    loop(ny + 1, 5, merid_second)

    pump(6)
    forward(5)
    ahead = 6
    thin = 8
    clane = lane_of((thin, nx))
    cfirst, clast = clane == 0, clane == nx - 1

    def zonal_part(c, rim, rim_value, speeds):
        diff = c - jnp.where(cfirst, rim, lanes(c, 1))
        ahead = jnp.where(clast, rim - c, lanes(diff, -1))
        half = 0.5 * minmod(diff, ahead)
        left, right = c + half, c - half
        before = jnp.where(cfirst, rim_value, lanes(left, 1))
        after = jnp.where(clast, rim_value, lanes(right, -1))
        return (speeds[2] * left + speeds[3] * after) - (speeds[0] * before + speeds[1] * right)

    def slide(values, take):
        c, d, h, f = [], [None], [None], [None]

        def push(x, speeds):
            c.append(x)
            i = len(c) - 1
            if i >= 1:
                d.append(c[i] - c[i - 1])
            if i >= 2:
                h.append(0.5 * minmod(d[i - 1], d[i]))
            if i >= 3:
                plus, minus = speeds(i - 3)
                f.append(plus * (c[i - 2] + h[i - 2]) + minus * (c[i - 1] - h[i - 1]))
            if i >= 4:
                take(i - 4, c[i - 2], f[i - 2] - f[i - 3])

        values(push)

    def tracer(t, carry):
        for side in (0, 1):
            arrives = there[1 - 2 * side]
            if relay:
                arrives = jnp.logical_and(arrives, jnp.logical_not(forwards(side)))

            @pl.when(arrives)
            def _(side=side):
                tracer_copy(side, t).wait_recv()
        for side in (0, 1):
            around[side] = halo_tr[side, t].astype(F32)
        back = nx - (GROUP * t + GROUP // 2)

        def levels(zc):
            zs = pl.ds(zc * thin, thin)
            start = []

            def second(push):
                def take(j, mid, along_y):
                    rim = pltpu.roll(m1[j, zs], back, 1)
                    rim_value = pltpu.roll(z1[j, zs], back, 1)
                    div = zonal_part(mid, rim, rim_value, [ua[k, j, zs] for k in range(4)]) + along_y
                    new = (mid - div).astype(BF16).astype(F32)
                    if j < 2:
                        new = in_south * new
                    if j >= ny + 2:
                        new = in_north * new
                    push(new, lambda k: (vb[0, k, zs], vb[1, k, zs]))

                def first(push_start):
                    for i in range(ny + 2 * HALO):
                        if i < HALO:
                            x = around[1, spot(i + ny - HALO, zc * thin, thin), :]
                        elif i < HALO + ny:
                            x = plain[t, spot(i - HALO, zc * thin, thin), :]
                        else:
                            x = around[0, spot(i - HALO - ny, zc * thin, thin), :]
                        start.append(x)
                        push_start(x, lambda k: (va[0, k, zs], va[1, k, zs]))

                slide(first, take)

            def finish(j, mid, along_y):
                rim = pltpu.roll(m2[j, zs], back, 1)
                rim_value = pltpu.roll(z2[j, zs], back, 1)
                div = zonal_part(mid, rim, rim_value, [ub[k, j, zs] for k in range(4)]) + along_y
                tt[t, j, zs] = 0.5 * (start[j + HALO] + mid) - div

            slide(second, finish)

        for zc in range(nz // thin):
            levels(zc)
        if relay:
            @pl.when(t + ahead < ntr)
            def _():
                forward(t + ahead)
        return carry

    lax.fori_loop(0, ntr, tracer, 0)

    for copy in inputs[2:]:
        copy.wait()
    chunk = 16
    block = lane_of((1, nx)) // WBX

    def wet_row(row):
        total = jnp.zeros((1, nx), F32)
        for k in range(nx // WBX):
            total = jnp.where(block == k, wet[row // WBY, k].astype(F32), total)
        return total

    def react(row):
        mask = react_step * wet_row(row)

        for zc in range(nz // chunk):
            zs = pl.ds(zc * chunk, chunk)
            x = [tt[t, row, zs] for t in range(ntr)]
            for a in range(ntr):
                total = rates[a, 0] * x[0]
                for b in range(1, ntr):
                    total = total + rates[a, b] * x[b]
                reacted = x[a] + mask * total
                plain[a, spot(row, zc * chunk, chunk), :] = reacted
                if a == 0:
                    tt[0, row, zs] = water_atten + chloro_atten * reacted * reacted

    loop(ny, 2, react)

    def fold(t):
        tr_out[t] = plain[t].astype(BF16)

    loop(ntr, 2, fold)
    results[4].start()

    def heat(row):
        att = tt[0, row]
        cum = depth_sum(att)
        heating = (wet_row(row) * light[pl.ds(row, 1), :]) * (jnp.exp(att - cum) - jnp.exp(-cum))
        heat_out[spot(row), :] = heating
        oc_out[2, spot(row), :] = oc_out[2, spot(row), :] + time_step * heating

    loop(ny, 4, heat)
    results[2].start()
    results[5].start()

    for index, (dy, dx) in enumerate(DIRS):
        @pl.when(has(dy, dx))
        def _(dy=dy, dx=dx, index=index):
            edge_copy(dy, dx, index).wait_send()
    for side in (0, 1):
        @pl.when(there[2 * side - 1])
        def _(side=side):
            ocean_copy(side).wait_send()

        @pl.when(sends(side))
        def _(side=side):
            for t in range(pumped, ntr):
                tracer_copy(side, t).wait_send()

        if relay:
            @pl.when(forwards(side))
            def _(side=side):
                for t in range(ntr):
                    forward_copy(side, t).wait_send()
    for copy in results:
        copy.wait()


def hand_out(ocean, tracers, heat, ocean_out, tracers_out, heat_out, ocean_held, tracers_held, heat_held, in_sem, out_sem):
    pieces = [(ocean.at[f], ocean_held.at[f], ocean_out.at[f]) for f in range(ocean.shape[0])]
    pieces += [(heat, heat_held, heat_out)]
    half = tracers.shape[0] // 2
    for part in (pl.ds(0, half), pl.ds(half, tracers.shape[0] - half)):
        pieces.append((tracers.at[part], tracers_held.at[part], tracers_out.at[part]))
    loads = [pltpu.make_async_copy(p[0], p[1], in_sem.at[k]) for k, p in enumerate(pieces)]
    stores = [pltpu.make_async_copy(p[1], p[2], out_sem.at[k]) for k, p in enumerate(pieces)]
    for copy in loads:
        copy.start()
    for load, store in zip(loads, stores):
        load.wait()
        store.start()
    for copy in stores:
        copy.wait()


def shards(ngrp, ntile, ocean, tracers, wet_blocks, surface_light, rates):
    ntr, nz, ny, nx = tracers.shape
    hbm = pl.BlockSpec(memory_space=pltpu.HBM)
    level, flat = (nz, nx), (nz * ny, nx)
    outs = pl.pallas_call(
        functools.partial(kernel, ngrp, ntile, ny),
        out_shape=(
            jax.ShapeDtypeStruct((4,) + flat, F32),
            jax.ShapeDtypeStruct((ntr,) + flat, BF16),
            jax.ShapeDtypeStruct(flat, F32),
        ),
        in_specs=[hbm] * 5,
        out_specs=(hbm,) * 3,
        scratch_shapes=[
            pltpu.VMEM((4,) + flat, F32),
            pltpu.VMEM((ntr,) + flat, BF16),
            pltpu.VMEM(flat, F32),
            pltpu.SemaphoreType.DMA((6,)),
            pltpu.VMEM((ntr,) + flat, BF16),
            pltpu.VMEM((4,) + flat, F32),
            pltpu.SMEM(wet_blocks.shape, jnp.int32),
            pltpu.VMEM(surface_light.shape, F32),
            pltpu.SMEM(rates.shape, F32),
            pltpu.SemaphoreType.DMA((5,)),
            pltpu.VMEM((2, ntr) + flat, BF16),
            pltpu.VMEM((2, len(RIM)) + level, BF16),
            pltpu.VMEM((2, len(RIM)) + level, BF16),
            pltpu.VMEM((3, ny + 4) + level, BF16),
            pltpu.VMEM((2, ny + 4) + level, F32),
            pltpu.VMEM((2, 2, ny + 4) + level, F32),
            pltpu.VMEM((4, ny + 6) + level, F32),
            pltpu.VMEM((4, ny + 2) + level, F32),
            pltpu.VMEM((ny + 4,) + level, F32),
            pltpu.VMEM((ny + 4,) + level, F32),
            pltpu.VMEM((ny,) + level, F32),
            pltpu.VMEM((ny,) + level, F32),
            pltpu.VMEM((4, ny + 4) + level, F32),
            pltpu.VMEM((2, ny + 5) + level, F32),
            pltpu.VMEM((4, ny) + level, F32),
            pltpu.VMEM((2, ny + 1) + level, F32),
            pltpu.VMEM((ntr, ny) + level, F32),
            pltpu.VMEM((ntr,) + flat, F32),
            pltpu.VMEM((2,) + flat, F32),
            pltpu.SemaphoreType.DMA((len(DIRS),)),
            pltpu.SemaphoreType.DMA((len(DIRS),)),
            pltpu.SemaphoreType.DMA((2,)),
            pltpu.SemaphoreType.DMA((2,)),
            pltpu.SemaphoreType.DMA((2, ntr)),
            pltpu.SemaphoreType.DMA((2, ntr)),
            pltpu.SemaphoreType.DMA((ntr,)),
        ],
        compiler_params=pltpu.CompilerParams(
            collective_id=0, has_side_effects=True, vmem_limit_bytes=VMEM_GRANT
        ),
    )(tracers.reshape((ntr,) + flat), ocean.reshape((4,) + flat), wet_blocks, surface_light, rates)
    outs = pl.pallas_call(
        hand_out,
        out_shape=[jax.ShapeDtypeStruct(out.shape, out.dtype) for out in outs],
        in_specs=[hbm] * 3,
        out_specs=[hbm] * 3,
        scratch_shapes=[pltpu.VMEM(out.shape, out.dtype) for out in outs] + [pltpu.SemaphoreType.DMA((7,))] * 2,
        compiler_params=pltpu.CompilerParams(vmem_limit_bytes=VMEM_GRANT),
    )(*outs)
    return outs[0].reshape(ocean.shape), outs[1].reshape(tracers.shape), outs[2].reshape(ocean.shape[1:])


def solution(mesh):
    return jax.shard_map(
        functools.partial(shards, mesh.shape["grp"], mesh.shape["tile"]),
        mesh=mesh,
        in_specs=(
            P(None, None, "grp", "tile"),
            P(None, None, "grp", "tile"),
            P("grp", "tile"),
            P("grp", "tile"),
            P(),
        ),
        out_specs=(
            P(None, None, "grp", "tile"),
            P(None, None, "grp", "tile"),
            P(None, "grp", "tile"),
        ),
        check_vma=False,
    )
```
